128 devices in a mesh: section: 2 (over core), dp: 16 (over y, z), mp: 4 (over x).
Axes of the slice: x: 4, y: 4, z: 4, core: 2. Of those that a mesh axis runs over, the one named last changes fastest.
Arguments:
- inputs: bfloat16 [2, 2048, 768], P(None, 'dp'), may hold values from -6 to 6
- cotangent: bfloat16 [2, 2048, 768], P(None, 'dp'), may hold values from -6 to 6
- segments: int32 [2, 2048], P(None, 'dp'), may hold values from 0 to 2047, as said below
- buckets: int32 [128], replicated, may hold values from 0 to 31
- routes: int32 [2, 2, 2048, 2], P('section', None, 'dp'), may hold values from 0 to 31, all different within a row; in each aligned block of 128 rows (0 to 127, 128 to 255, ..., all dimensions but the last counted through in order) at most 16 rows name the same one
- gates: float32 [2, 2, 2048, 2], P('section', None, 'dp'), may hold values from 0.2 to 0.8
- attn_gain: bfloat16 [2, 768], P('section', 'dp'), may hold values from 0.5 to 1.5
- qkv_weight: bfloat16 [2, 768, 3, 768], P('section', 'dp', None, 'mp'), may hold values from -0.21875 to 0.21875
- out_weight: bfloat16 [2, 768, 768], P('section', 'dp', 'mp'), may hold values from -0.4375 to 0.4375
- rel_bias: bfloat16 [2, 32, 12], P('section', 'dp', 'mp'), may hold values from -4 to 4
- ffn_gain: bfloat16 [2, 768], P('section', 'dp'), may hold values from 0.5 to 1.5
- w_in: bfloat16 [2, 32, 768, 3072], P('section', 'dp', None, 'mp'), may hold values from -0.21875 to 0.21875
- w_out: bfloat16 [2, 32, 3072, 768], P('section', 'dp', 'mp'), may hold values from -0.15625 to 0.15625
Outputs:
- states: bfloat16 [2, 2, 2048, 768], P('section', None, 'dp')
- input_grads: bfloat16 [2, 2, 2048, 768], P('section', None, 'dp')
- attn_gain_grad: float32 [2, 768], P('section', 'dp')
- qkv_grad: float32 [2, 768, 3, 768], P('section', 'dp', None, 'mp')
- out_grad: float32 [2, 768, 768], P('section', 'dp', 'mp')
- rel_bias_grad: float32 [2, 32, 12], P('section', 'dp', 'mp')
- ffn_gain_grad: float32 [2, 768], P('section', 'dp')
- w_in_grad: float32 [2, 32, 768, 3072], P('section', 'dp', None, 'mp')
- w_out_grad: float32 [2, 32, 3072, 768], P('section', 'dp', 'mp')
The draws below stay inside these ranges and needn't reach their ends.
Inputs may be any that keep to these rules, and one draw needn't show every extreme that they name: `segments`: A token's id is the place of its sequence's first token in the row, so ids never fall along a row; a new sequence begins at every multiple of 128 and at the row's last token. `routes`: A row names two different experts; in each aligned block of 128 rows (one layer, one micro-batch, one index of dp) no expert is named by more than 16 rows.
All inputs are finite; a program needn't handle non-finite values.
Results may differ from the reference program's by a relative error of at most 0.039.
Values may be sent and summed in bfloat16 or wider, within the bound.
No kernel may reach another device: no remote copies, remote signals or barrier semaphores. Data moves between devices by JAX's collectives and lax.ppermute only.
A program may use at most 128 MiB of HBM per device.

```python
import math
import jax
import jax.numpy as jnp
import numpy as np
from jax import lax

D = 768
H = 12
DH = 64
FF = 3072
NB = 32
MB = 2
TOK_MB = 128
L = 2
TOKENS = 2048
EXPERTS = 32
CAP = 16
N_SECTION = 2
N_DP = 16


def draw_segments(key, part):
    key = jax.random.fold_in(key, 11)
    starts = jax.random.randint(key, (MB, TOKENS), 0, 24) == 0
    places = jnp.arange(TOKENS, dtype=jnp.int32)
    forced = (places % TOK_MB == 0) | (places == TOKENS - 1)
    starts = starts | forced[None, :]
    marks = jnp.where(starts, places[None, :], 0).astype(jnp.int32)
    return lax.cummax(marks, axis=1)


def set_ends(array, own_key, smallest, largest):
    spot = [jax.random.randint(jax.random.fold_in(own_key, axis), (), 0, length) for axis, length in enumerate(array.shape)]
    longest = array.shape.index(max(array.shape))
    beside = spot[:longest] + [(spot[longest] + 1) % array.shape[longest]] + spot[longest + 1:]
    return array.at[tuple(spot)].set(smallest).at[tuple(beside)].set(largest)


def levels(stream_key, dims, shards, low, largest):
    def one(dim, shards_of):
        steps = jax.random.uniform(jax.random.fold_in(jax.random.fold_in(stream_key, 6), dim), (shards_of,), jnp.float32, low / len(shards), largest / len(shards))
        return jnp.repeat(jnp.exp(steps), dims[dim] // shards_of).reshape((-1,) + (1,) * (len(dims) - dim - 1))

    factor_of = one(*shards[0])
    for cut in shards[1:]:
        factor_of = factor_of * one(*cut)
    return factor_of


def routed_block(own_key, own, number, rows, number_of, top, reach, lean):
    sequence = jax.random.permutation(own_key, number_of)
    heavy_load, usual = load_shares(number_of, rows * top, reach, lean, True), load_shares(number_of, rows * top, reach, lean, False)
    places = jnp.arange(number_of)

    def named(sizes, turn):
        used = int((sizes > 0).sum())
        fixed = max(1, used // 4)
        shifted = fixed + (places - fixed + turn * (used - fixed)) % max(1, number_of - fixed)
        return jnp.zeros((number_of,), jnp.int32).at[sequence[jnp.where(places < fixed, places, shifted)]].set(jnp.asarray(sizes, jnp.int32))

    sizes = jnp.where(number % 4 == 0, named(heavy_load, number // 4), named(usual, number - number // 4 - 1))
    mixed = jax.random.permutation(jax.random.fold_in(own, 3), number_of)
    giver, receiver = mixed[0:number_of // 2 * 2:2], mixed[1:number_of // 2 * 2:2]
    slack = jnp.minimum(sizes[giver] - 1, reach - sizes[receiver]) // 2
    slack = jnp.where((giver == sequence[0]) | (receiver == sequence[0]) | (sizes[receiver] == 0), 0, jnp.maximum(slack, 0))
    shifted = jax.random.randint(jax.random.fold_in(own, 4), (number_of // 2,), 0, 1 << 20) % (slack + 1)
    sizes = sizes.at[giver].add(-shifted).at[receiver].add(shifted)
    members = jnp.searchsorted(jnp.cumsum(sizes), jnp.arange(rows * top), side="right").astype(jnp.int32)
    listing = members.reshape(top, rows).T
    listing = listing[jax.random.permutation(jax.random.fold_in(own, 1), rows)]
    turn = jax.random.randint(jax.random.fold_in(own, 2), (rows, 1), 0, top)
    return jnp.take_along_axis(listing, (jnp.arange(top)[None, :] + turn) % top, axis=1)


def load_shares(amount, total, bound, skew, full):
    loads = [(1 << 20) // math.isqrt(standing ** skew) + 1 for standing in range(1, amount + 1)]
    largest = bound if full else min(bound, max(-(-total // amount), total * loads[0] // sum(loads)))
    least = 1 if total - largest >= amount - 1 else 0
    holding, surplus = [largest] + [least] * (amount - 1), total - largest - least * (amount - 1)
    while surplus > 0:
        candidates = [i for i in range(1, amount) if holding[i] < largest] or [i for i in range(1, amount) if holding[i] < bound]
        mass, budget = sum([loads[i] for i in candidates]), surplus
        for i in candidates:
            more = min(bound - holding[i], max(1, budget * loads[i] // mass), surplus)
            holding[i] = holding[i] + more
            surplus = surplus - more
    return np.array(holding)


def scatter_about(own_key, extent, scale, most, shards=(), held_as=jnp.bfloat16):
    values = scale * jax.random.normal(own_key, extent, jnp.float32)
    if shards:
        values = values * levels(own_key, extent, shards, -0.22, 0.18)
    return jnp.clip(values, -most, most).astype(held_as)


def setup_inputs(seed: int = 0) -> dict:
    seeds = jax.random.split(jax.random.key(seed), 14)
    inputs = scatter_about(seeds[0], (MB, TOKENS, D), 1.0, 6.0, ((1, 16),))
    cotangent = scatter_about(seeds[1], (MB, TOKENS, D), 1.0, 6.0, ((1, 16),))
    segments = draw_segments(jax.random.fold_in(seeds[13], 71), 0)
    buckets = set_ends(jax.random.randint(seeds[3], (TOK_MB,), 0, NB), jax.random.fold_in(seeds[3], 1), 0, NB - 1).astype(jnp.int32)
    routes_keys = jax.random.split(jax.random.fold_in(seeds[4], 1), L * MB * TOKENS // TOK_MB)
    routes_turns = jax.random.permutation(jax.random.fold_in(seeds[4], 3), L * MB * TOKENS // TOK_MB)
    routes = jax.vmap(lambda own, number: routed_block(jax.random.fold_in(seeds[4], 2), own, number, TOK_MB, EXPERTS, 2, CAP, 1))(routes_keys, routes_turns).reshape((L, MB, TOKENS, 2))
    gates = jnp.clip(0.2 + 0.6 * jax.random.uniform(seeds[5], (L, MB, TOKENS, 2), jnp.float32) ** levels(seeds[5], (L, MB, TOKENS, 2), ((0, 2), (2, 16)), -0.2, 0.2), 0.2, 0.8)
    attn_gain = jnp.clip(1.0 + 0.1 * jax.random.normal(seeds[6], (L, D), jnp.float32), 0.5, 1.5).astype(jnp.bfloat16)
    qkv_weight = scatter_about(seeds[7], (L, D, 3, H * DH), D ** -0.5, 0.21875, ((0, 2), (1, 16), (3, 4)))
    out_weight = scatter_about(seeds[8], (L, D, H * DH), (H * DH // 4) ** -0.5, 0.4375, ((0, 2), (1, 16), (2, 4)))
    rel_bias = scatter_about(seeds[9], (L, NB, H), 1.0, 4.0, ((0, 2), (1, 16), (2, 4)))
    ffn_gain = jnp.clip(1.0 + 0.1 * jax.random.normal(seeds[10], (L, D), jnp.float32), 0.5, 1.5).astype(jnp.bfloat16)
    w_in = scatter_about(seeds[11], (L, EXPERTS, D, FF), D ** -0.5, 0.21875, ((0, 2), (1, 16), (3, 4)))
    w_out = scatter_about(seeds[12], (L, EXPERTS, FF, D), (FF // 2) ** -0.5, 0.15625, ((0, 2), (1, 16), (2, 4)))
    return {"inputs": inputs, "cotangent": cotangent, "segments": segments, "buckets": buckets, "routes": routes, "gates": gates, "attn_gain": attn_gain, "qkv_weight": qkv_weight, "out_weight": out_weight, "rel_bias": rel_bias, "ffn_gain": ffn_gain, "w_in": w_in, "w_out": w_out}


@jax.custom_vjp
def low(v):
    return lax.optimization_barrier(v.astype(jnp.bfloat16)).astype(jnp.float32)

@jax.custom_vjp
def low_back(v):
    return v

def low_keep(v):
    return (low(v), None)

def low_pass(kept, grad):
    return (grad,)

def back_keep(v):
    return (v, None)

def back_low(kept, grad):
    return (low(grad),)
low.defvjp(low_keep, low_pass)
low_back.defvjp(back_keep, back_low)
epsilon = 1e-06
highest = lax.Precision.HIGHEST
negative = -1e+30

def rms_norm(values, gain):
    return values * lax.rsqrt(lax.optimization_barrier(jnp.mean(values * values, axis=-1, keepdims=True)) + epsilon) * gain

def slot_table(route):
    flat = route.reshape(N_DP, TOK_MB * 2)
    onehot = (flat[:, :, None] == jnp.arange(EXPERTS, dtype=jnp.int32)[None, None, :]).astype(jnp.int32)
    earlier = jnp.cumsum(onehot, axis=1) - onehot
    position = lax.optimization_barrier(jnp.sum(earlier * onehot, axis=2))
    block = jnp.arange(N_DP, dtype=jnp.int32)[:, None]
    return ((flat * N_DP + block) * CAP + position).reshape(TOKENS * 2)

def layer(hidden, segment, route, gate, weights, causal, bucket_grid):
    attn_gain, qkv_weight, out_weight, rel_bias, ffn_gain, w_in, w_out = weights
    hidden = low_back(hidden)
    normed = low(rms_norm(hidden, attn_gain))
    proj = low(low_back(jnp.einsum('td,dcf->ctf', normed, qkv_weight, precision=highest)))
    split = proj.reshape(3, N_DP, TOK_MB, H, DH)
    bias = jnp.transpose(rel_bias[bucket_grid], (2, 0, 1))
    blocks = segment.reshape(N_DP, TOK_MB)
    mask = causal[None] & (blocks[:, :, None] == blocks[:, None, :])
    raw = jnp.einsum('bqhe,bkhe->bhqk', split[0], split[1], precision=highest) * 0.125 + bias[None]
    scores = jnp.where(mask[:, None], low_back(raw), negative)
    peak = lax.optimization_barrier(jnp.max(scores, axis=-1, keepdims=True))
    expos = jnp.exp(scores - peak)
    probs = low(expos / lax.optimization_barrier(jnp.sum(expos, axis=-1, keepdims=True)))
    context = low(low_back(jnp.einsum('bhqk,bkhe->bqhe', probs, split[2], precision=highest)))
    context = context.reshape(TOKENS, H * DH)
    middle = hidden + low_back(jnp.einsum('tf,df->td', context, out_weight, precision=highest))
    normed_two = low(rms_norm(middle, ffn_gain))
    slots = slot_table(route)
    buffer = jnp.zeros((EXPERTS * N_DP * CAP, D), jnp.float32).at[slots].set(jnp.repeat(normed_two, 2, axis=0))
    buffer = low_back(buffer).reshape(EXPERTS, N_DP * CAP, D)
    before = low_back(jnp.einsum('erd,edf->erf', buffer, w_in, precision=highest))
    active = low(jax.nn.gelu(before))
    rows = low(low_back(jnp.einsum('erf,efd->erd', active, w_out, precision=highest)))
    picked = rows.reshape(EXPERTS * N_DP * CAP, D)[slots].reshape(TOKENS, 2, D)
    return low(middle + lax.optimization_barrier(jnp.sum(gate[:, :, None] * picked, axis=1)))

def make_apply(route, gate, segments, causal, bucket_grid):
    step_fn = jax.checkpoint(layer)

    def apply(value, weights):
        outputs = [step_fn(value[number], segments[number], route[number], gate[number], weights, causal, bucket_grid) for number in range(MB)]
        return jnp.stack(outputs)
    return apply

def reference(inputs, cotangent, segments, buckets, routes, gates, attn_gain, qkv_weight, out_weight, rel_bias, ffn_gain, w_in, w_out):
    places = jnp.arange(TOK_MB, dtype=jnp.int32)
    distance = places[:, None] - places[None, :]
    causal = distance >= 0
    bucket_grid = buckets[jnp.clip(distance, 0, TOK_MB - 1)]
    stacks = [param.astype(jnp.float32) for param in (attn_gain, qkv_weight, out_weight, rel_bias, ffn_gain, w_in, w_out)]
    value = inputs.astype(jnp.float32)
    pulls = []
    states = []
    for layer_index in range(N_SECTION):
        weights = tuple((stack[layer_index] for stack in stacks))
        apply = make_apply(routes[layer_index], gates[layer_index], segments, causal, bucket_grid)
        value, pull = jax.vjp(apply, value, weights)
        states.append(value)
        pulls.append(pull)
    grad = cotangent.astype(jnp.float32)
    input_grads = [None] * N_SECTION
    weight_grads = [None] * N_SECTION
    for layer_index in reversed(range(N_SECTION)):
        grad, weight_grads[layer_index] = pulls[layer_index](grad)
        input_grads[layer_index] = grad
    gathered = [jnp.stack([weight_grads[layer_index][which] for layer_index in range(N_SECTION)]) for which in range(7)]
    return (jnp.stack(states).astype(jnp.bfloat16), jnp.stack(input_grads).astype(jnp.bfloat16), gathered[0], gathered[1], gathered[2], gathered[3], gathered[4], gathered[5], gathered[6])
```

```python
import functools

import jax
import jax.numpy as jnp
from jax import lax
from jax.experimental import pallas as pl
from jax.experimental.pallas import tpu as pltpu
from jax.sharding import PartitionSpec as P

bf16 = jnp.bfloat16
f32 = jnp.float32
epsilon = 1e-06
negative = -1e30
root = 0.7978845608028654
cubic = 0.044715
TOK = 128
WIDTH = 768
HEADS = 3
DH = 64
SPLIT = 192
PACK = 896
SLOTS = 512
CAP = 16


def dot(a, b):
    return lax.dot_general(a, b, (((1,), (0,)), ((), ())), preferred_element_type=f32)


def dot_nt(a, b):
    return lax.dot_general(a, b, (((1,), (1,)), ((), ())), preferred_element_type=f32)


def dot_tn(a, b):
    return lax.dot_general(a, b, (((0,), (0,)), ((), ())), preferred_element_type=f32)


def iota(shape, dim):
    return lax.broadcasted_iota(jnp.int32, shape, dim)


def norm_scale(values):
    return lax.rsqrt(jnp.mean(values * values, axis=-1, keepdims=True) + epsilon)


def swapped(x):
    return lax.ppermute(x, "section", [(0, 1), (1, 0)])


def sent(x, source):
    return lax.ppermute(x, "section", [(source, 1 - source)])


def call(kernel, outs, any_args=(), scalars=1, scratch=(), args=(), name=None):
    specs = []
    for index in range(len(args)):
        if index < scalars:
            specs.append(pl.BlockSpec(memory_space=pltpu.SMEM))
        elif index in any_args:
            specs.append(pl.BlockSpec(memory_space=pl.ANY))
        else:
            specs.append(pl.BlockSpec(memory_space=pltpu.VMEM))
    return pl.pallas_call(
        kernel,
        out_shape=[jax.ShapeDtypeStruct(shape, dtype) for shape, dtype in outs],
        in_specs=specs,
        out_specs=[pl.BlockSpec(memory_space=pltpu.VMEM) for _ in outs],
        scratch_shapes=list(scratch),
        compiler_params=pltpu.CompilerParams(vmem_limit_bytes=48 * 1024 * 1024),
        name=name,
    )(*args)


def fetch(here, own, other, buffer, sems):
    count = buffer.shape[0]

    @pl.when(here)
    def _():
        for i in range(count):
            pltpu.make_async_copy(own.at[i], buffer.at[i], sems.at[i]).start()

    @pl.when(jnp.logical_not(here))
    def _():
        for i in range(count):
            pltpu.make_async_copy(other.at[i], buffer.at[i], sems.at[i]).start()

    def arrived(i):
        pltpu.make_async_copy(own.at[i], buffer.at[i], sems.at[i]).wait()

    return arrived


def prepare_kernel(ids, own, other, segments, cotangent, pick, gated, mask, sent_grad):
    section = ids[0]
    first = section == 0
    row = jnp.where(first, segments[0:1, :], segments[1:2, :]).astype(f32)
    column = own[:, 0:1]
    causal = iota((TOK, TOK), 0) >= iota((TOK, TOK), 1)
    mask[...] = jnp.where(causal & (column == row), 1.0, 0.0)
    expert = iota((TOK, 32), 1).astype(f32)
    lower = jnp.where(iota((TOK, TOK), 0) > iota((TOK, TOK), 1), 1.0, 0.0).astype(bf16)
    spread = jnp.where(lax.shift_right_logical(iota((32, SLOTS), 1), 4) == iota((32, SLOTS), 0), 1.0, 0.0).astype(bf16)
    slot = iota((TOK, SLOTS), 1)
    slot_expert = lax.shift_right_logical(slot, 4).astype(f32)
    slot_place = (slot & 15).astype(f32)
    for layer in range(2):
        info = jnp.where(section == layer, own[...], other[...])
        r0, r1, g0, g1 = info[:, 1:2], info[:, 2:3], info[:, 3:4], info[:, 4:5]
        named = jnp.where((r0 == expert) | (r1 == expert), 1.0, 0.0).astype(bf16)
        earlier = dot(lower, named)
        here = dot(earlier.astype(bf16), spread) == slot_place
        d0 = here & (r0 == slot_expert)
        d1 = here & (r1 == slot_expert)
        pick[layer] = jnp.where(d0 | d1, 1.0, 0.0).astype(bf16)
        gates = jnp.where(d0, g0, jnp.where(d1, g1, 0.0)).astype(bf16)
        gated[layer] = gates
        if layer == 1:
            grad = jnp.where(first, cotangent[0], cotangent[1])
            sent_grad[...] = dot_tn(gates, grad).astype(bf16)


def gains(chunk):
    rows = chunk.astype(f32).T
    return rows[0:1], rows[1:2]


def attend(count, arrived, weights, normed, onehot, allowed, proj_out, probs_out, context_out):
    total = None
    for part in range(count):
        arrived(part)
        proj = dot(normed, weights[part, :, : 3 * SPLIT]).astype(bf16)
        proj_out[part] = proj
        line = dot_tn(weights[part, :, WIDTH:], onehot).astype(bf16)
        pieces = []
        for head in range(HEADS):
            at = head * DH
            query = proj[:, at : at + DH]
            key = proj[:, SPLIT + at : SPLIT + at + DH]
            value = proj[:, 2 * SPLIT + at : 2 * SPLIT + at + DH]
            chosen = jnp.where(iota((TOK, TOK), 1) == 2 + head, 1.0, 0.0).astype(bf16)
            bias = pltpu.roll(dot(chosen, line), 0, 1, stride=1, stride_axis=0)
            scores = jnp.where(allowed, dot_nt(query, key) * 0.125 + bias, negative)
            peak = jnp.max(scores, axis=-1, keepdims=True)
            expos = jnp.exp(scores - peak)
            probs = (expos / jnp.sum(expos, axis=-1, keepdims=True)).astype(bf16)
            probs_out[part * HEADS + head] = probs
            pieces.append(dot(probs, value).astype(bf16))
        context = jnp.concatenate(pieces, axis=1)
        context_out[part] = context
        padded = jnp.concatenate([jnp.zeros((TOK, DH), bf16), context], axis=1)
        term = dot_nt(padded, weights[part, :, 512:WIDTH])
        total = term if total is None else total + term
    return total


def forward_kernel(layer, ids, *refs):
    if layer == 0:
        inputs, own, other, onehot, mask, pick = refs[:6]
        rest = refs[6:]
    else:
        before, parts, own, other, onehot, mask, pick = refs[:7]
        rest = refs[7:]
        state_out, rest = rest[0], rest[1:]
    sent_out, middle_out, normed_out, proj_out, probs_out, context_out, weights, sems = rest
    section = ids[0]
    arrived = fetch(section == layer, own, other, weights, sems)
    if layer == 0:
        hidden = jnp.where(section == 0, inputs[0], inputs[1]).astype(f32)
    else:
        added = parts[0].astype(f32)
        for i in range(1, 4):
            added = added + parts[i].astype(f32)
        state = (before[...] + added).astype(bf16)
        state_out[...] = state
        hidden = state.astype(f32)
    scaled = hidden * norm_scale(hidden)
    arrived_first = arrived

    arrived_first(0)
    gain_one, gain_two = gains(weights[0, :, WIDTH:])

    def wait(part):
        if part > 0:
            arrived(part)

    normed = (scaled * gain_one).astype(bf16)
    normed_out[...] = normed
    allowed = mask[...] > 0.5
    attn = attend(4, wait, weights, normed, onehot[...], allowed, proj_out, probs_out, context_out)
    middle = hidden + attn
    middle_out[...] = middle
    normed_two = (middle * norm_scale(middle) * gain_two).astype(bf16)
    sent_out[...] = dot_tn(pick[layer], normed_two).astype(bf16)


def gelu_both(x):
    square = x * x
    th = jnp.tanh(root * (x + cubic * x * square))
    half = 0.5 * (1.0 + th)
    value = x * half
    slope = half + 0.5 * x * (1.0 - th * th) * (root * (1.0 + 3.0 * cubic * square))
    return value, slope


def rows_of(ref, expert):
    return ref[:, expert].reshape(256, WIDTH)


def expert_kernel(mode, layer, ids, *refs):
    if mode == "forward":
        received, in_own, in_other, out_own, out_other, y_out, act_out, slope_out = refs[:8]
    elif mode == "both":
        received, arrived_grad, in_own, in_other, out_own, out_other, y_out, buf_out, act_out, pre_out = refs[:10]
    else:
        arrived_grad, slope_in, in_own, in_other, out_own, out_other, buf_out, pre_out = refs[:8]
    w_in, w_out, in_sems, out_sems = refs[-4:]
    here = ids[0] == layer
    in_arrived = fetch(here, in_own, in_other, w_in, in_sems)
    out_arrived = fetch(here, out_own, out_other, w_out, out_sems)
    for e in range(2):
        in_arrived(e)
        if mode != "backward":
            value, slope = gelu_both(dot(rows_of(received, e), w_in[e]))
            act = value.astype(bf16)
            act_out[e] = act
            out_arrived(e)
            y_out[:, e] = dot(act, w_out[e]).astype(bf16).reshape(16, CAP, WIDTH)
            if mode == "forward":
                slope_out[e] = slope.astype(bf16)
        else:
            out_arrived(e)
            slope = slope_in[e].astype(f32)
        if mode != "forward":
            pre = (dot_nt(rows_of(arrived_grad, e), w_out[e]) * slope).astype(bf16)
            pre_out[e] = pre
            buf_out[:, e] = dot_nt(pre, w_in[e]).astype(bf16).reshape(16, CAP, WIDTH)


def combine_kernel(layer, matrix, returned, out):
    out[...] = dot(matrix[layer], returned[...]).astype(bf16)


def state_kernel(before, parts, out):
    added = parts[0].astype(f32)
    for i in range(1, 4):
        added = added + parts[i].astype(f32)
    out[...] = (before[...] + added).astype(bf16)


def backward_kernel(layer, ids, *refs):
    if layer == 1:
        grads, hidden_ref = refs[0], refs[1]
    else:
        grads, hidden_ref = refs[0], refs[1]
    parts, middle_ref, proj_ref, probs_ref, own, other, onehot = refs[2:9]
    rest = refs[9:]
    if layer == 1:
        gated, rest = rest[0], rest[1:]
    grad_out, rest = rest[0], rest[1:]
    if layer == 1:
        sent_out, rest = rest[0], rest[1:]
    attn_out, proj_grad_out, small_out, weights, all_proj, all_scores, sems = rest
    section = ids[0]
    device = ids[1]
    arrived = fetch(section == layer, own, other, weights, sems)
    first = section == 0
    if layer == 1:
        grad = jnp.where(first, grads[0], grads[1]).astype(f32)
        hidden = hidden_ref[...].astype(f32)
    else:
        grad = grads[...].astype(f32)
        hidden = jnp.where(first, hidden_ref[0], hidden_ref[1]).astype(f32)
    middle = middle_ref[...]
    buf = parts[0].astype(f32)
    for i in range(1, 4):
        buf = buf + parts[i].astype(f32)
    scale_two = norm_scale(middle)
    arrived(0)
    gain_one, gain_two = gains(weights[0, :, WIDTH:])
    small_out[...] = jnp.zeros(small_out.shape, f32)
    unit = middle * scale_two
    small_out[1:2, :] = jnp.sum(buf * unit, axis=0, keepdims=True)
    inner = jnp.mean(unit * gain_two * buf, axis=-1, keepdims=True)
    middle_grad = grad + scale_two * (gain_two * buf - unit * inner)
    attn_low = middle_grad.astype(bf16)
    attn_out[...] = attn_low
    normed_grad = None
    for part in range(4):
        if part > 0:
            arrived(part)
        context_grad = dot(attn_low, weights[part, :, 512:WIDTH]).astype(bf16)
        proj = proj_ref[part]
        q_parts, k_parts, v_parts = [], [], []
        for head in range(HEADS):
            at = head * DH
            query = proj[:, at : at + DH]
            key = proj[:, SPLIT + at : SPLIT + at + DH]
            value = proj[:, 2 * SPLIT + at : 2 * SPLIT + at + DH]
            probs = probs_ref[part * HEADS + head]
            back = context_grad[:, DH + at : DH + at + DH]
            wide = probs.astype(f32)
            prob_grad = dot_nt(back, value)
            inner = jnp.sum(wide * prob_grad, axis=-1, keepdims=True)
            score_grad = (wide * (prob_grad - inner)).astype(bf16)
            all_scores[part * HEADS + head] = score_grad
            q_parts.append(dot(score_grad, key) * 0.125)
            k_parts.append(dot_tn(score_grad, query) * 0.125)
            v_parts.append(dot_tn(probs, back))
        proj_grad = jnp.concatenate(q_parts + k_parts + v_parts, axis=1).astype(bf16)
        all_proj[part] = proj_grad
        term = dot_nt(proj_grad, weights[part, :, : 3 * SPLIT])
        normed_grad = term if normed_grad is None else normed_grad + term
    scale_one = norm_scale(hidden)
    unit = hidden * scale_one
    small_out[0:1, :] = jnp.sum(normed_grad * unit, axis=0, keepdims=True)
    inner = jnp.mean(unit * gain_one * normed_grad, axis=-1, keepdims=True)
    low = (middle_grad + scale_one * (gain_one * normed_grad - unit * inner)).astype(bf16)
    grad_out[...] = low
    if layer == 1:
        sent_out[...] = dot_tn(gated[0], low).astype(bf16)
    proj_grad_out[...] = all_proj[device]
    flip = jnp.where(iota((TOK, TOK), 0) + iota((TOK, TOK), 1) == TOK - 1, 1.0, 0.0).astype(bf16)
    for head in range(HEADS):
        flipped = dot(flip, all_scores[device * HEADS + head])
        lined = pltpu.roll(flipped, 1, 1, stride=1, stride_axis=0)
        small_out[2 + head : 3 + head, 0:TOK] = jnp.sum(lined, axis=0, keepdims=True)


def weight_grad_kernel(ids, *refs):
    layers = (refs[0:10], refs[10:20])
    onehot, out = refs[20], refs[21]
    section = ids[0]
    device = ids[1]
    for layer in range(2):

        @pl.when(section == layer)
        def _(layer=layer):
            normed, proj_grad, attn, context, small, normed2, proj_grad2, attn2, context2, small2 = layers[layer]
            out[:, : 3 * SPLIT] = (
                dot_tn(normed[...], proj_grad[...]) + dot_tn(normed2[...], proj_grad2[...])
            ).astype(bf16)
            out[:, 3 * SPLIT : WIDTH] = (
                dot_tn(attn[...], context[device]) + dot_tn(attn2[...], context2[device])
            ).astype(bf16)
            rows = small[...] + small2[...]
            lines = rows[:, 0:TOK].astype(bf16)
            keep = (iota((TOK, 16), 1) >= 2) & (iota((TOK, 16), 1) < 5) & (iota((TOK, 16), 0) == iota((TOK, 16), 1))
            lines = dot(jnp.where(keep, 1.0, 0.0).astype(bf16), lines).astype(bf16)
            table = dot_nt(onehot[...], lines)
            tall = jnp.concatenate([rows, jnp.zeros((TOK - 16, WIDTH), f32)], axis=0).T
            lane = iota((WIDTH, TOK), 1)
            out[:, WIDTH:] = jnp.where(lane < 2, tall, table).astype(bf16)


def sum_kernel(received, out):
    total = received[0].astype(f32)
    for i in range(1, received.shape[0]):
        total = total + received[i].astype(f32)
    out[...] = total


def expert_grad_kernel(ids, *refs):
    layers = (refs[0:8], refs[8:16])
    in_out, out_out = refs[16], refs[17]
    buffers = refs[18:26]
    sems = refs[26]
    expert = pl.program_id(0)
    section = ids[0]

    @pl.when(expert == 0)
    def _():
        for layer in range(2):

            @pl.when(section == layer)
            def _(layer=layer):
                for i in range(8):
                    pltpu.make_async_copy(layers[layer][i], buffers[i], sems.at[i]).start()

        for i in range(8):
            pltpu.make_async_copy(layers[0][i], buffers[i], sems.at[i]).wait()

    received, act, pre, arrived, received2, act2, pre2, arrived2 = buffers
    rows = received[:, expert].reshape(256, WIDTH)
    rows2 = received2[:, expert].reshape(256, WIDTH)
    in_out[0] = dot_tn(rows, pre[expert]) + dot_tn(rows2, pre2[expert])
    grads = arrived[:, expert].reshape(256, WIDTH)
    grads2 = arrived2[:, expert].reshape(256, WIDTH)
    out_out[0] = dot_tn(act[expert], grads) + dot_tn(act2[expert], grads2)


def exchanged(x):
    return lax.all_to_all(x.reshape(16, -1, x.shape[-1]), "dp", 0, 0, tiled=True)


def gathered_mp(x):
    return lax.all_gather(x, "mp", axis=0)


def body(
    inputs, cotangent, segments, buckets, routes, gates, attn_gain, qkv_weight, out_weight, rel_bias, ffn_gain, w_in, w_out
):
    section = lax.axis_index("section")
    ids = jnp.stack([section, lax.axis_index("mp")]).astype(jnp.int32)
    pack = jnp.concatenate(
        [
            qkv_weight.reshape(48, 3 * SPLIT),
            out_weight.reshape(48, SPLIT),
            attn_gain.reshape(48, 1),
            ffn_gain.reshape(48, 1),
            jnp.pad(rel_bias[0], ((0, 46), (0, 0))),
            jnp.zeros((48, PACK - WIDTH - 5), bf16),
        ],
        axis=1,
    )
    w_own = lax.all_gather(pack, ("mp", "dp"), axis=0).reshape(4, WIDTH, PACK)
    w_other = swapped(w_own)
    in_own, out_own = w_in[0], w_out[0]
    in_other, out_other = swapped(in_own), swapped(out_own)
    info = jnp.concatenate(
        [segments.astype(f32)[:, :, None], routes[0].astype(f32), gates[0], jnp.zeros((2, TOK, 3), f32)], axis=2
    )
    info_own = lax.dynamic_index_in_dim(info, section, 0, False)
    info_other = swapped(lax.dynamic_index_in_dim(info, 1 - section, 0, False))
    reverse = jnp.concatenate([buckets[0:1], buckets[1:][::-1]])
    place = jnp.arange(WIDTH, dtype=jnp.int32)
    number = jnp.where(place % 48 < 2, 2 * (place // 48) + place % 48, -1)
    onehot = (number[:, None] == reverse[None, :]).astype(bf16)

    pick, gated, mask, grad_sent = call(
        prepare_kernel,
        [((2, TOK, SLOTS), bf16), ((2, TOK, SLOTS), bf16), ((TOK, TOK), f32), ((SLOTS, WIDTH), bf16)],
        args=(ids, info_own, info_other, segments, cotangent),
        name="prepare",
    )
    blocks = (16, 2, CAP, WIDTH)
    arrived_one = exchanged(grad_sent).reshape(blocks)

    kept_shapes = [
        ((SLOTS, WIDTH), bf16),
        ((TOK, WIDTH), f32),
        ((TOK, WIDTH), bf16),
        ((4, TOK, 3 * SPLIT), bf16),
        ((12, TOK, TOK), bf16),
        ((4, TOK, SPLIT), bf16),
    ]
    weight_scratch = [pltpu.VMEM((4, WIDTH, PACK), bf16)]
    sems4 = [pltpu.SemaphoreType.DMA((4,))]
    sent_zero, middle_zero, normed_zero, proj_zero, probs_zero, context_zero = call(
        functools.partial(forward_kernel, 0),
        kept_shapes,
        any_args=(2, 3),
        scratch=weight_scratch + sems4,
        args=(ids, inputs, w_own, w_other, onehot, mask, pick),
        name="attention_zero",
    )
    received_zero = exchanged(sent_zero).reshape(blocks)
    expert_scratch = [
        pltpu.VMEM((2, WIDTH, WIDTH), bf16),
        pltpu.VMEM((2, WIDTH, WIDTH), bf16),
        pltpu.SemaphoreType.DMA((2,)),
        pltpu.SemaphoreType.DMA((2,)),
    ]
    hidden_shape = ((2, 256, WIDTH), bf16)
    y_zero, act_zero, slope_zero = call(
        functools.partial(expert_kernel, "forward", 0),
        [(blocks, bf16), hidden_shape, hidden_shape],
        any_args=(2, 3, 4, 5),
        scratch=expert_scratch,
        args=(ids, received_zero, in_own, in_other, out_own, out_other),
        name="experts_zero",
    )
    token_shape = ((TOK, WIDTH), bf16)

    def combined(layer, matrix, rows, name):
        back = exchanged(rows).reshape(SLOTS, WIDTH)
        part = call(
            functools.partial(combine_kernel, layer), [token_shape], scalars=0, args=(matrix, back), name=name
        )[0]
        return gathered_mp(part)

    parts_zero = combined(0, gated, y_zero, "combine_zero")
    state_zero, sent_one, middle_one, normed_one, proj_one, probs_one, context_one = call(
        functools.partial(forward_kernel, 1),
        [token_shape] + kept_shapes,
        any_args=(3, 4),
        scratch=weight_scratch + sems4,
        args=(ids, middle_zero, parts_zero, w_own, w_other, onehot, mask, pick),
        name="attention_one",
    )
    received_one = exchanged(sent_one).reshape(blocks)
    y_one, buf_one, act_one, pre_one = call(
        functools.partial(expert_kernel, "both", 1),
        [(blocks, bf16), (blocks, bf16), hidden_shape, hidden_shape],
        any_args=(3, 4, 5, 6),
        scratch=expert_scratch,
        args=(ids, received_one, arrived_one, in_own, in_other, out_own, out_other),
        name="experts_one",
    )
    buf_parts_one = combined(1, pick, buf_one, "combine_back_one")
    y_parts_one = combined(1, gated, y_one, "combine_one")
    state_one = call(
        state_kernel, [token_shape], scalars=0, args=(middle_one, y_parts_one), name="state_one"
    )[0]
    grad_scratch = weight_scratch + [pltpu.VMEM((4, TOK, 3 * SPLIT), bf16), pltpu.VMEM((12, TOK, TOK), bf16)] + sems4
    grad_shapes = [token_shape, ((TOK, 3 * SPLIT), bf16), ((16, WIDTH), f32)]
    grad_one, grad_sent_zero, attn_grad_one, proj_grad_one, small_one = call(
        functools.partial(backward_kernel, 1),
        [token_shape, ((SLOTS, WIDTH), bf16)] + grad_shapes,
        any_args=(7, 8),
        scratch=grad_scratch,
        args=(
            ids, cotangent, state_zero, buf_parts_one, middle_one, proj_one, probs_one, w_own, w_other, onehot, gated
        ),
        name="attention_back_one",
    )
    arrived_zero = exchanged(grad_sent_zero).reshape(blocks)
    buf_zero, pre_zero = call(
        functools.partial(expert_kernel, "backward", 0),
        [(blocks, bf16), hidden_shape],
        any_args=(3, 4, 5, 6),
        scratch=expert_scratch,
        args=(ids, arrived_zero, slope_zero, in_own, in_other, out_own, out_other),
        name="experts_back_zero",
    )
    buf_parts_zero = combined(0, pick, buf_zero, "combine_back_zero")
    grad_zero, attn_grad_zero, proj_grad_zero, small_zero = call(
        functools.partial(backward_kernel, 0),
        [token_shape] + grad_shapes,
        any_args=(7, 8),
        scratch=grad_scratch,
        args=(ids, grad_one, inputs, buf_parts_zero, middle_zero, proj_zero, probs_zero, w_own, w_other, onehot),
        name="attention_back_zero",
    )

    def with_peer(arrays, source):
        return tuple(arrays) + tuple(sent(x, source) for x in arrays)

    experts_zero = with_peer((received_zero, act_zero, pre_zero, arrived_zero), 1)
    experts_one = with_peer((received_one, act_one, pre_one, arrived_one), 0)
    in_grad, out_grad = pl.pallas_call(
        expert_grad_kernel,
        out_shape=[jax.ShapeDtypeStruct((2, WIDTH, WIDTH), f32)] * 2,
        grid=(2,),
        in_specs=[pl.BlockSpec(memory_space=pltpu.SMEM)] + [pl.BlockSpec(memory_space=pl.ANY)] * 16,
        out_specs=[pl.BlockSpec((1, WIDTH, WIDTH), lambda e: (e, 0, 0))] * 2,
        scratch_shapes=[
            pltpu.VMEM(shape, bf16) for _ in range(2) for shape in (blocks, (2, 256, WIDTH), (2, 256, WIDTH), blocks)
        ]
        + [pltpu.SemaphoreType.DMA((8,))],
        compiler_params=pltpu.CompilerParams(vmem_limit_bytes=48 * 1024 * 1024),
        name="expert_grads",
    )(ids, *experts_zero, *experts_one)

    layer_zero = with_peer((normed_zero, proj_grad_zero, attn_grad_zero, context_zero, small_zero), 1)
    layer_one = with_peer((normed_one, proj_grad_one, attn_grad_one, context_one, small_one), 0)
    packed = call(
        weight_grad_kernel,
        [((WIDTH, PACK), bf16)],
        args=(ids, *layer_zero, *layer_one, onehot),
        name="attention_grads",
    )[0]
    shares = exchanged(packed.reshape(16, 48, PACK))
    total = call(sum_kernel, [((48, PACK), f32)], scalars=0, args=(shares,), name="sum_grads")[0]

    def outputs(zero, one):
        mine = jnp.where(section == 0, zero, one)
        peer = swapped(jnp.where(section == 0, one, zero))
        return jnp.where(section == 0, jnp.stack([mine, peer]), jnp.stack([peer, mine]))[None]

    states = outputs(state_zero, state_one)
    input_grads = outputs(grad_zero, grad_one)
    return (
        states,
        input_grads,
        total[:, WIDTH].reshape(1, 48),
        total[:, : 3 * SPLIT].reshape(1, 48, 3, SPLIT),
        total[:, 3 * SPLIT : WIDTH].reshape(1, 48, SPLIT),
        total[0:2, WIDTH + 2 : WIDTH + 5].reshape(1, 2, 3),
        total[:, WIDTH + 1].reshape(1, 48),
        in_grad[None],
        out_grad[None],
    )


def solution(mesh):
    return jax.shard_map(
        body,
        mesh=mesh,
        in_specs=(
            P(None, "dp", None),
            P(None, "dp", None),
            P(None, "dp"),
            P(),
            P("section", None, "dp", None),
            P("section", None, "dp", None),
            P("section", "dp"),
            P("section", "dp", None, "mp"),
            P("section", "dp", "mp"),
            P("section", "dp", "mp"),
            P("section", "dp"),
            P("section", "dp", None, "mp"),
            P("section", "dp", "mp", None),
        ),
        out_specs=(
            P("section", None, "dp", None),
            P("section", None, "dp", None),
            P("section", "dp"),
            P("section", "dp", None, "mp"),
            P("section", "dp", "mp"),
            P("section", "dp", "mp"),
            P("section", "dp"),
            P("section", "dp", None, "mp"),
            P("section", "dp", "mp", None),
        ),
        check_vma=False,
    )
```

```python
import functools

import jax
import jax.numpy as jnp
from jax import lax
from jax.experimental import pallas as pl
from jax.experimental.pallas import tpu as pltpu
from jax.sharding import PartitionSpec as P

bf16 = jnp.bfloat16
f32 = jnp.float32
epsilon = 1e-06
negative = -1e30
root = 0.7978845608028654
cubic = 0.044715
TOK = 128
WIDTH = 768
HEADS = 3
DH = 64
SPLIT = 192
PACK = 896
SLOTS = 512
CAP = 16


def dot(a, b):
    return lax.dot_general(a, b, (((1,), (0,)), ((), ())), preferred_element_type=f32)


def dot_nt(a, b):
    return lax.dot_general(a, b, (((1,), (1,)), ((), ())), preferred_element_type=f32)


def dot_tn(a, b):
    return lax.dot_general(a, b, (((0,), (0,)), ((), ())), preferred_element_type=f32)


def iota(shape, dim):
    return lax.broadcasted_iota(jnp.int32, shape, dim)


def norm_scale(values):
    return lax.rsqrt(jnp.mean(values * values, axis=-1, keepdims=True) + epsilon)


def swapped(x):
    return lax.ppermute(x, "section", [(0, 1), (1, 0)])


def sent(x, source):
    return lax.ppermute(x, "section", [(source, 1 - source)])


class Loaded:
    def __init__(self, source, buffer, sem):
        self.copy = pltpu.make_async_copy(source, buffer, sem)
        self.buffer, self.waiting = buffer, True
        self.copy.start()

    def ready(self):
        if self.waiting:
            self.copy.wait()
            self.waiting = False

    def __getitem__(self, index):
        self.ready()
        return self.buffer[index]


class Stored:
    def __init__(self, target, buffer, sems):
        self.target, self.buffer, self.sems, self.copies = target, buffer, sems, []
        self.dtype = target.dtype

    def __setitem__(self, index, value):
        self.buffer[index] = value

    def start(self, *index):
        source = self.buffer.at[index] if index else self.buffer
        target = self.target.at[index] if index else self.target
        copy = pltpu.make_async_copy(source, target, self.sems.at[len(self.copies)])
        copy.start()
        self.copies.append(copy)

    def finish(self):
        for copy in self.copies:
            copy.wait()


def far(x):
    return pltpu.with_memory_space_constraint(x, pltpu.HBM)


def call(kernel, outs, raw=(), load=(), store=(), scalars=1, scratch=(), args=(), name=None, limit=16):
    specs = []
    for index in range(len(args)):
        if index < scalars:
            specs.append(pl.BlockSpec(memory_space=pltpu.SMEM))
        elif index in raw or index in load:
            specs.append(pl.BlockSpec(memory_space=pltpu.HBM))
        else:
            specs.append(pl.BlockSpec(memory_space=pltpu.VMEM))
    extra = [pltpu.VMEM(args[i].shape, args[i].dtype) for i in load]
    extra += [pltpu.VMEM(*outs[i]) for i in store]
    if load:
        extra.append(pltpu.SemaphoreType.DMA((len(load),)))
    if store:
        extra.append(pltpu.SemaphoreType.DMA((len(store), 8)))

    def wrapped(*refs):
        refs = list(refs)
        count = len(args) + len(outs)
        own = refs[count : len(refs) - len(extra)]
        more = refs[len(refs) - len(extra) :]
        load_sems = more[len(load) + len(store)] if load else None
        store_sems = more[-1] if store else None
        for n, i in enumerate(load):
            refs[i] = Loaded(refs[i], more[n], load_sems.at[n])
        stored = []
        for n, i in enumerate(store):
            refs[len(args) + i] = Stored(refs[len(args) + i], more[len(load) + n], store_sems.at[n])
            stored.append(refs[len(args) + i])
        kernel(*refs[:count], *own)
        for item in refs[:count]:
            if isinstance(item, Loaded):
                item.ready()
        for item in stored:
            if not item.copies:
                item.start()
        for item in stored:
            item.finish()

    args = [far(x) if i in raw or i in load else x for i, x in enumerate(args)]
    return pl.pallas_call(
        wrapped,
        out_shape=[
            pltpu.HBM(shape, dtype) if i in store else jax.ShapeDtypeStruct(shape, dtype)
            for i, (shape, dtype) in enumerate(outs)
        ],
        in_specs=specs,
        out_specs=[
            pl.BlockSpec(memory_space=pltpu.HBM if i in store else pltpu.VMEM) for i in range(len(outs))
        ],
        scratch_shapes=list(scratch) + extra,
        compiler_params=pltpu.CompilerParams(vmem_limit_bytes=limit * 1024 * 1024),
        name=name,
    )(*args)


def fetch(here, own, other, buffer, sems):
    count = buffer.shape[0]

    @pl.when(here)
    def _():
        for i in range(count):
            pltpu.make_async_copy(own.at[i], buffer.at[i], sems.at[i]).start()

    @pl.when(jnp.logical_not(here))
    def _():
        for i in range(count):
            pltpu.make_async_copy(other.at[i], buffer.at[i], sems.at[i]).start()

    def arrived():
        for i in range(count):
            pltpu.make_async_copy(own.at[i], buffer.at[i], sems.at[i]).wait()

    return arrived


def pack_kernel(qkv, out_part, gain_one, gain_two, table, whole, halves):
    eye = iota((48, 48), 0) == iota((48, 48), 1)
    one = jnp.sum(jnp.where(eye, gain_one[...].astype(f32), 0.0), axis=1, keepdims=True)
    two = jnp.sum(jnp.where(eye, gain_two[...].astype(f32), 0.0), axis=1, keepdims=True)
    row, lane = iota((48, TOK), 0), iota((48, TOK), 1)
    extra = jnp.where(lane == 0, one, jnp.where(lane == 1, two, 0.0))
    values = table[...].astype(f32)
    for r in range(2):
        for h in range(HEADS):
            extra = extra + jnp.where((row == r) & (lane == 2 + h), values[r : r + 1, h : h + 1], 0.0)
    parts = [qkv[0], qkv[1], qkv[2], out_part[...]]
    line = jnp.concatenate(parts + [extra.astype(bf16), jnp.zeros((48, TOK), bf16)], axis=1)
    whole[...] = line[:, :PACK]
    halves[0] = line[:, :512]
    halves[1] = line[:, 512:]


def spread_kernel(ids, halves, received, out):
    chosen = jnp.where(ids[0] == 0, halves[0], received[...])
    for i in range(16):
        out[i] = chosen


def first_kernel(ids, inputs, own, other, onehot, mask, part_out, gains_out):
    first = ids[0] == 0
    hidden = jnp.where(first, inputs[0], inputs[1]).astype(f32)
    scaled = hidden * norm_scale(hidden)
    low = jnp.where(first, own[...], other[...])
    high = jnp.where(first, other[...], own[...])
    weight = jnp.concatenate([low, high], axis=1)
    rows = weight[:, WIDTH:PACK].astype(f32).T
    gains_out[...] = rows[0:8]
    normed = (scaled * rows[0:1]).astype(bf16)
    proj = dot(normed, weight[:, : 3 * SPLIT]).astype(bf16)
    line = dot_tn(weight[:, WIDTH:PACK], onehot[...]).astype(bf16)
    allowed = mask[...] > 0.5
    pieces = [jnp.zeros((TOK, DH), bf16)]
    for head in range(HEADS):
        probs, value = head_probs(proj, head_bias(line, allowed, head), head)
        pieces.append(dot(probs, value).astype(bf16))
    part_out[...] = dot_nt(jnp.concatenate(pieces, axis=1), weight[:, 512:WIDTH]).astype(bf16)


def dispatch_kernel(ids, inputs, parts, gain_rows, pick, middle_out, sent_out):
    hidden = jnp.where(ids[0] == 0, inputs[0], inputs[1]).astype(f32)
    for i in range(4):
        hidden = hidden + parts[i].astype(f32)
    middle_out[...] = hidden
    normed = (hidden * norm_scale(hidden) * gain_rows[1:2, :]).astype(bf16)
    sent_out[...] = dot_tn(pick[...], normed).astype(bf16)


def prepare_kernel(ids, own, other, segments, cotangent, pick_zero, pick_one, gated_zero, gated_one, mask, sent_grad):
    section = ids[0]
    first = section == 0
    row = jnp.where(first, segments[0:1, :], segments[1:2, :]).astype(f32)
    column = own[:, 0:1]
    causal = iota((TOK, TOK), 0) >= iota((TOK, TOK), 1)
    mask[...] = jnp.where(causal & (column == row), 1.0, 0.0)
    expert = iota((TOK, 32), 1).astype(f32)
    lower = jnp.where(iota((TOK, TOK), 0) > iota((TOK, TOK), 1), 1.0, 0.0).astype(bf16)
    spread = jnp.where(lax.shift_right_logical(iota((32, SLOTS), 1), 4) == iota((32, SLOTS), 0), 1.0, 0.0).astype(bf16)
    slot = iota((TOK, SLOTS), 1)
    slot_expert = lax.shift_right_logical(slot, 4).astype(f32)
    slot_place = (slot & 15).astype(f32)
    for layer in range(2):
        info = jnp.where(section == layer, own[...], other[...])
        r0, r1, g0, g1 = info[:, 1:2], info[:, 2:3], info[:, 3:4], info[:, 4:5]
        named = jnp.where((r0 == expert) | (r1 == expert), 1.0, 0.0).astype(bf16)
        earlier = dot(lower, named)
        here = dot(earlier.astype(bf16), spread) == slot_place
        d0 = here & (r0 == slot_expert)
        d1 = here & (r1 == slot_expert)
        (pick_zero, pick_one)[layer][...] = jnp.where(d0 | d1, 1.0, 0.0).astype(bf16)
        gates = jnp.where(d0, g0, jnp.where(d1, g1, 0.0)).astype(bf16)
        (gated_zero, gated_one)[layer][...] = gates
        if layer == 1:
            grad = jnp.where(first, cotangent[0], cotangent[1])
            sent_grad[...] = dot_tn(gates, grad).astype(bf16)


def head_bias(line, allowed, head):
    chosen = jnp.where(iota((TOK, TOK), 1) == 2 + head, 1.0, 0.0).astype(bf16)
    bias = pltpu.roll(dot(chosen, line), 0, 1, stride=1, stride_axis=0)
    return jnp.where(allowed, bias, negative)


def head_probs(proj, bias, head):
    at = head * DH
    query = proj[:, at : at + DH]
    key = proj[:, SPLIT + at : SPLIT + at + DH]
    value = proj[:, 2 * SPLIT + at : 2 * SPLIT + at + DH]
    scores = dot_nt(query * jnp.asarray(0.125, bf16), key) + bias
    peak = jnp.max(scores, axis=-1, keepdims=True)
    expos = jnp.exp(scores - peak)
    return (expos / jnp.sum(expos, axis=-1, keepdims=True)).astype(bf16), value


def bias_kernel(layer, ids, own, other, onehot, mask, bias_out, gains_out, extra, sem):
    lanes = pl.ds(WIDTH, TOK)

    @pl.when(ids[0] == layer)
    def _():
        pltpu.make_async_copy(own.at[:, :, lanes], extra, sem).start()

    @pl.when(ids[0] != layer)
    def _():
        pltpu.make_async_copy(other.at[:, :, lanes], extra, sem).start()

    pltpu.make_async_copy(own.at[:, :, lanes], extra, sem).wait()
    gains_out[...] = extra[0].astype(f32).T[0:8]
    allowed = mask[...] > 0.5
    for part in range(4):
        line = dot_tn(extra[part], onehot[...]).astype(bf16)
        for head in range(HEADS):
            bias_out[part * HEADS + head] = head_bias(line, allowed, head).astype(bf16)


def forward_kernel(layer, ids, *refs):
    if layer == 0:
        inputs, own, other, gain_rows, bias = refs[:5]
        rest = refs[5:]
    else:
        before, parts, own, other, gain_rows, bias, pick, state_out, sent_out, middle_out = refs[:10]
        rest = refs[10:]
    normed_out, proj_out, probs_out, context_out, contexts, weights, sems = rest
    section = ids[0]
    arrived = fetch(section == layer, own, other, weights, sems)
    if layer == 0:
        hidden = jnp.where(section == 0, inputs[0], inputs[1]).astype(f32)
    else:
        added = parts[0].astype(f32)
        for i in range(1, 4):
            added = added + parts[i].astype(f32)
        state = (before[...] + added).astype(bf16)
        state_out[...] = state
        state_out.start()
        hidden = state.astype(f32)
    normed = (hidden * norm_scale(hidden) * gain_rows[0:1, :]).astype(bf16)
    normed_out[...] = normed
    normed_out.start()
    attn = None
    arrived()
    for part in range(4):
        proj = dot(normed, weights[part, :, : 3 * SPLIT]).astype(bf16)
        proj_out[part] = proj
        proj_out.start(part)
        pieces = []
        for head in range(HEADS):
            probs, value = head_probs(proj, bias[part * HEADS + head].astype(f32), head)
            probs_out[part * HEADS + head] = probs
            pieces.append(dot(probs, value).astype(bf16))
        probs_out.start(pl.ds(part * HEADS, HEADS))
        contexts[part] = jnp.concatenate(pieces, axis=1)
        if layer == 1:
            padded = jnp.concatenate([jnp.zeros((TOK, DH), bf16)] + pieces, axis=1)
            term = dot_nt(padded, weights[part, :, 512:WIDTH])
            attn = term if attn is None else attn + term
    context_out[...] = contexts[ids[1]]
    context_out.start()
    if layer == 1:
        middle = hidden + attn
        middle_out[...] = middle
        middle_out.start()
        normed_two = (middle * norm_scale(middle) * gain_rows[1:2, :]).astype(bf16)
        sent_out[...] = dot_tn(pick[...], normed_two).astype(bf16)


def gelu_both(x):
    square = x * x
    th = jnp.tanh(root * (x + cubic * x * square))
    half = 0.5 * (1.0 + th)
    value = x * half
    slope = half + 0.5 * x * (1.0 - th * th) * (root * (1.0 + 3.0 * cubic * square))
    return value, slope


def rows_of(ref, expert):
    return ref[:, expert].reshape(256, WIDTH)


def expert_kernel(mode, layer, ids, *refs):
    if mode == "forward":
        received, in_own, in_other, out_own, out_other, y_out, ahead, slope_out = refs[:8]
    elif mode == "both":
        received, arrived_grad, in_own, in_other, out_own, out_other, y_out, buf_out, ahead, behind = refs[:10]
    else:
        slope_in, arrived_grad, in_own, in_other, out_own, out_other, buf_out, behind = refs[:8]
    w_in, w_out, in_sems, out_sems = refs[-4:]
    in_arrived = fetch(ids[0] == layer, in_own, in_other, w_in, in_sems)
    out_arrived = fetch(ids[0] == layer, out_own, out_other, w_out, out_sems)
    in_arrived()
    out_arrived()
    for e in range(2):
        if mode != "backward":
            rows = rows_of(received, e)
            value, slope = gelu_both(dot(rows, w_in[e]))
            act = value.astype(bf16)
            ahead[0, e] = rows
            ahead[1, e] = act
            ahead.start(slice(None), e)
            y_out[:, e] = dot(act, w_out[e]).astype(bf16).reshape(16, CAP, WIDTH)
            if mode == "forward":
                slope_out[e] = slope.astype(bf16)
                slope_out.start(e)
        else:
            slope = slope_in[e].astype(f32)
        if mode != "forward":
            back = rows_of(arrived_grad, e)
            pre = (dot_nt(back, w_out[e]) * slope).astype(bf16)
            behind[0, e] = pre
            behind[1, e] = back
            behind.start(slice(None), e)
            buf_out[:, e] = dot_nt(pre, w_in[e]).astype(bf16).reshape(16, CAP, WIDTH)


def combine_kernel(matrix, returned, out):
    out[...] = dot(matrix[...], returned[...]).astype(out.dtype)


def state_kernel(ids, before, *refs):
    parts, out, ordered = refs[:4], refs[4], refs[5]
    for by in range(4):
        ordered[(ids[1] + 4 - by) & 3] = parts[by][...]
    total = before[...]
    for i in range(4):
        total = total + ordered[i].astype(f32)
    out[...] = total.astype(bf16)


def backward_kernel(layer, ids, *refs):
    if layer == 1:
        grads, hidden_ref = refs[0], refs[1]
    else:
        grads, hidden_ref = refs[0], refs[1]
    parts, middle_ref, proj_ref, probs_ref, own, other, gain_rows, normed_ref, context_ref = refs[2:11]
    rest = refs[11:]
    if layer == 1:
        gated, rest = rest[0], rest[1:]
    if layer == 1:
        sent_out, rest = rest[0], rest[1:]
    bundle, all_proj, all_scores, small_out, weights, sems = rest
    arrived = fetch(ids[0] == layer, own, other, weights, sems)
    section = ids[0]
    device = ids[1]
    first = section == 0
    if layer == 1:
        grad = jnp.where(first, grads[0], grads[1]).astype(f32)
        hidden = hidden_ref[...].astype(f32)
    else:
        grad = grads[3 * TOK : 4 * TOK].astype(f32)
        hidden = jnp.where(first, hidden_ref[0], hidden_ref[1]).astype(f32)
    middle = middle_ref[...]
    buf = parts[0].astype(f32)
    for i in range(1, 4):
        buf = buf + parts[i].astype(f32)
    scale_two = norm_scale(middle)
    gain_one, gain_two = gain_rows[0:1, :], gain_rows[1:2, :]
    small_out[...] = jnp.zeros(small_out.shape, f32)
    unit = middle * scale_two
    small_out[1:2, :] = jnp.sum(buf * unit, axis=0, keepdims=True)
    inner = jnp.mean(unit * gain_two * buf, axis=-1, keepdims=True)
    middle_grad = grad + scale_two * (gain_two * buf - unit * inner)
    attn_low = middle_grad.astype(bf16)
    bundle[0:TOK] = normed_ref[...]
    bundle[TOK : 2 * TOK] = attn_low
    normed_grad = None
    arrived()
    for part in range(4):
        context_grad = dot(attn_low, weights[part, :, 512:WIDTH]).astype(bf16)
        proj = proj_ref[part]
        q_parts, k_parts, v_parts = [], [], []
        for head in range(HEADS):
            at = head * DH
            query = proj[:, at : at + DH]
            key = proj[:, SPLIT + at : SPLIT + at + DH]
            value = proj[:, 2 * SPLIT + at : 2 * SPLIT + at + DH]
            probs = probs_ref[part * HEADS + head]
            back = context_grad[:, DH + at : DH + at + DH]
            wide = probs.astype(f32)
            prob_grad = dot_nt(back, value)
            inner = jnp.sum(wide * prob_grad, axis=-1, keepdims=True)
            score_grad = (wide * (prob_grad - inner)).astype(bf16)
            all_scores[part * HEADS + head] = score_grad
            q_parts.append(dot(score_grad, key) * 0.125)
            k_parts.append(dot_tn(score_grad, query) * 0.125)
            v_parts.append(dot_tn(probs, back))
        proj_grad = jnp.concatenate(q_parts + k_parts + v_parts, axis=1).astype(bf16)
        all_proj[part] = proj_grad
        term = dot_nt(proj_grad, weights[part, :, : 3 * SPLIT])
        normed_grad = term if normed_grad is None else normed_grad + term
    scale_one = norm_scale(hidden)
    unit = hidden * scale_one
    small_out[0:1, :] = jnp.sum(normed_grad * unit, axis=0, keepdims=True)
    inner = jnp.mean(unit * gain_one * normed_grad, axis=-1, keepdims=True)
    low = (middle_grad + scale_one * (gain_one * normed_grad - unit * inner)).astype(bf16)
    bundle[3 * TOK : 4 * TOK] = low
    if layer == 1:
        sent_out[...] = dot_tn(gated[...], low).astype(bf16)
    bundle[2 * TOK : 3 * TOK] = jnp.concatenate([all_proj[device], context_ref[...]], axis=1)
    flip = jnp.where(iota((TOK, TOK), 0) + iota((TOK, TOK), 1) == TOK - 1, 1.0, 0.0).astype(bf16)
    for head in range(HEADS):
        flipped = dot(flip, all_scores[device * HEADS + head])
        lined = pltpu.roll(flipped, 1, 1, stride=1, stride_axis=0)
        small_out[2 + head : 3 + head, 0:TOK] = jnp.sum(lined, axis=0, keepdims=True)
    bundle[4 * TOK :] = small_out[...].astype(bf16)


def weight_grad_kernel(ids, zero, zero_peer, one, one_peer, onehot, out):
    one.ready()
    one_peer.ready()
    for layer, (mine, peer) in enumerate(((zero, zero_peer), (one, one_peer))):

        @pl.when(ids[0] == layer)
        def _(mine=mine, peer=peer):
            both = [jnp.concatenate([mine[i * TOK : i * TOK + TOK], peer[i * TOK : i * TOK + TOK]], axis=0) for i in range(3)]
            normed, attn, third = both
            left = dot_tn(normed, third[:, : 3 * SPLIT])
            right = dot_tn(attn, third[:, 3 * SPLIT :])
            rows = mine[4 * TOK :].astype(f32) + peer[4 * TOK :].astype(f32)
            lines = rows[:, 0:TOK].astype(bf16)
            keep = (iota((TOK, 16), 1) >= 2) & (iota((TOK, 16), 1) < 5) & (iota((TOK, 16), 0) == iota((TOK, 16), 1))
            lines = dot(jnp.where(keep, 1.0, 0.0).astype(bf16), lines).astype(bf16)
            table = dot_nt(onehot[...], lines)
            tall = jnp.concatenate([rows, jnp.zeros((TOK - 16, WIDTH), f32)], axis=0).T
            lane = iota((WIDTH, TOK), 1)
            extra = jnp.where(lane < 2, tall, table)
            out[...] = jnp.concatenate([left, right, extra], axis=1).astype(bf16).reshape(16, 48, PACK)


def sum_kernel(received, qkv, out_part, extra):
    total = received[0].astype(f32)
    for i in range(1, 16):
        total = total + received[i].astype(f32)
    for c in range(3):
        qkv[c] = total[:, c * SPLIT : (c + 1) * SPLIT]
    out_part[...] = total[:, 3 * SPLIT : WIDTH]
    extra[...] = total[:, WIDTH:].T[0:8, :]


def assemble_kernel(ids, state_zero, state_one, state_zero_peer, state_one_peer, zero, one, zero_peer, one_peer, states, grads):
    rows = slice(3 * TOK, 4 * TOK)
    for item in (state_zero, state_zero_peer, state_one_peer, zero, one, zero_peer, one_peer):
        item.ready()

    @pl.when(ids[0] == 0)
    def _():
        states[0] = state_zero[...]
        states[1] = state_zero_peer[...]
        grads[0] = zero[rows]
        grads[1] = zero_peer[rows]

    @pl.when(ids[0] == 1)
    def _():
        states[0] = state_one_peer[...]
        states[1] = state_one[...]
        grads[0] = one_peer[rows]
        grads[1] = one[rows]


def expert_grad_kernel(ids, *refs):
    layers = (refs[0:4], refs[4:8])
    in_out, out_out, buffer, sems = refs[8:]
    expert = pl.program_id(0)

    @pl.when(expert == 0)
    def _():
        for layer, sources in enumerate(layers):

            @pl.when(ids[0] == layer)
            def _(sources=sources):
                for e in range(2):
                    for i, source in enumerate(sources):
                        pltpu.make_async_copy(source.at[:, e], buffer.at[i, :, e], sems.at[e, i]).start()

    for e in range(2):

        @pl.when(expert == e)
        def _(e=e):
            for i, source in enumerate(layers[0]):
                pltpu.make_async_copy(source.at[:, e], buffer.at[i, :, e], sems.at[e, i]).wait()

    rows, act = [jnp.concatenate([buffer[0, i, expert], buffer[2, i, expert]], axis=0) for i in range(2)]
    pre, back = [jnp.concatenate([buffer[1, i, expert], buffer[3, i, expert]], axis=0) for i in range(2)]
    in_out[0] = dot_tn(rows, pre)
    out_out[0] = dot_tn(act, back)


def after(x, *earlier):
    return lax.optimization_barrier((x, *earlier))[0]


def exchanged(x):
    return lax.all_to_all(x.reshape(16, -1, x.shape[-1]), "dp", 0, 0, tiled=True)


def gathered_mp(x):
    return lax.all_gather(x, "mp", axis=0)


def body(
    inputs, cotangent, segments, buckets, routes, gates, attn_gain, qkv_weight, out_weight, rel_bias, ffn_gain, w_in, w_out
):
    section = lax.axis_index("section")
    ids = jnp.stack([section, lax.axis_index("mp")]).astype(jnp.int32)
    pack, halves = call(
        pack_kernel,
        [((48, PACK), bf16), ((2, 48, 512), bf16)],
        scalars=0,
        load=(0, 1, 2, 3, 4),
        args=(qkv_weight[0].transpose(1, 0, 2), out_weight[0], attn_gain, ffn_gain, rel_bias[0]),
        name="pack",
    )
    spread = call(
        spread_kernel, [((16, 48, 512), bf16)], args=(ids, halves, sent(halves[1], 0)), name="spread"
    )[0]
    w_own = lax.all_gather(pack, ("mp", "dp"), axis=0).reshape(4, WIDTH, PACK)
    in_own, out_own = w_in[0], w_out[0]
    in_other, out_other = swapped(after(in_own, spread)), swapped(after(out_own, spread))
    info = jnp.concatenate(
        [segments.astype(f32)[:, :, None], routes[0].astype(f32), gates[0], jnp.zeros((2, TOK, 3), f32)], axis=2
    )
    info_own = lax.dynamic_index_in_dim(info, section, 0, False)
    info_other = swapped(lax.dynamic_index_in_dim(info, 1 - section, 0, False))
    reverse = jnp.concatenate([buckets[0:1], buckets[1:][::-1]])
    place = jnp.arange(WIDTH, dtype=jnp.int32)
    number = jnp.where(place % 48 < 2, 2 * (place // 48) + place % 48, -1)
    onehot = (number[:, None] == reverse[None, :]).astype(bf16)

    choice = ((TOK, SLOTS), bf16)
    token_shape = ((TOK, WIDTH), bf16)
    sent_shape = ((SLOTS, WIDTH), bf16)
    middle_shape = ((TOK, WIDTH), f32)
    gain_shape = ((8, WIDTH), f32)
    pick_zero, pick_one, gated_zero, gated_one, mask, grad_sent = call(
        prepare_kernel,
        [choice, choice, choice, choice, ((TOK, TOK), f32), sent_shape],
        load=(4,),
        args=(ids, info_own, info_other, segments, cotangent),
        name="prepare",
    )
    half_own = after(exchanged(spread).reshape(WIDTH, 512), mask)
    half_other = swapped(half_own)
    blocks = (16, 2, CAP, WIDTH)
    arrived_one = exchanged(grad_sent).reshape(blocks)
    part_zero, gains_zero = call(
        first_kernel,
        [token_shape, gain_shape],
        load=(1,),
        args=(ids, inputs, half_own, half_other, onehot, mask),
        name="first",
    )
    middle_zero, sent_zero = call(
        dispatch_kernel,
        [middle_shape, sent_shape],
        load=(1,),
        store=(0,),
        args=(ids, inputs, after(gathered_mp(part_zero), arrived_one), gains_zero, pick_zero),
        name="dispatch_zero",
    )
    pair_shape = ((2, 2, 256, WIDTH), bf16)
    received_zero = exchanged(sent_zero).reshape(blocks)
    weights = (in_own, in_other, out_own, out_other)
    expert_scratch = [
        pltpu.VMEM((2, WIDTH, WIDTH), bf16),
        pltpu.VMEM((2, WIDTH, WIDTH), bf16),
        pltpu.SemaphoreType.DMA((2,)),
        pltpu.SemaphoreType.DMA((2,)),
    ]
    y_zero, ahead_zero, slope_zero = call(
        functools.partial(expert_kernel, "forward", 0),
        [(blocks, bf16), pair_shape, ((2, 256, WIDTH), bf16)],
        raw=(2, 3, 4, 5),
        store=(1, 2),
        scratch=expert_scratch,
        args=(ids, received_zero, *weights),
        name="experts_zero",
        limit=20,
    )
    w_own = after(w_own, y_zero)
    w_other = swapped(w_own)

    def combined(matrix, back, name):
        return call(
            combine_kernel, [token_shape], scalars=0, args=(matrix, back.reshape(SLOTS, WIDTH)), name=name
        )[0]

    bias_shape = ((12, TOK, TOK), bf16)
    bias_scratch = [pltpu.VMEM((4, WIDTH, TOK), bf16), pltpu.SemaphoreType.DMA]

    def biased(layer, name):
        return call(
            functools.partial(bias_kernel, layer),
            [bias_shape, gain_shape],
            raw=(1, 2),
            store=(0,),
            scratch=bias_scratch,
            args=(ids, w_own, w_other, onehot, mask),
            name=name,
        )

    bias_one, gains_one = biased(1, "bias_one")
    y_back_zero = after(exchanged(y_zero), gains_one)
    parts_zero = gathered_mp(combined(gated_zero, y_back_zero, "combine_zero"))
    kept_shapes = [token_shape, ((4, TOK, 3 * SPLIT), bf16), bias_shape, ((TOK, SPLIT), bf16)]
    weight_scratch = [pltpu.VMEM((4, WIDTH, PACK), bf16), pltpu.SemaphoreType.DMA((4,))]
    forward_scratch = [pltpu.VMEM((4, TOK, SPLIT), bf16)] + weight_scratch
    state_zero, sent_one, middle_one, normed_one, proj_one, probs_one, context_one = call(
        functools.partial(forward_kernel, 1),
        [token_shape, sent_shape, middle_shape] + kept_shapes,
        raw=(3, 4),
        load=(1, 6),
        store=(0, 2, 3, 4, 5, 6),
        scratch=forward_scratch,
        args=(ids, middle_zero, parts_zero, w_own, w_other, gains_one, bias_one, pick_one),
        name="attention_one",
        limit=20,
    )
    bias_zero = biased(0, "bias_zero")[0]
    normed_zero, proj_zero, probs_zero, context_zero = call(
        functools.partial(forward_kernel, 0),
        kept_shapes,
        raw=(2, 3),
        load=(1, 5),
        store=(0, 1, 2, 3),
        scratch=forward_scratch,
        args=(ids, inputs, w_own, after(w_other, sent_one), gains_zero, bias_zero),
        name="attention_zero",
        limit=20,
    )
    received_one = after(exchanged(sent_one).reshape(blocks), normed_zero)
    y_one, buf_one, ahead_one, behind_one = call(
        functools.partial(expert_kernel, "both", 1),
        [(blocks, bf16), (blocks, bf16), pair_shape, pair_shape],
        raw=(3, 4, 5, 6),
        store=(2, 3),
        scratch=expert_scratch,
        args=(ids, received_one, arrived_one, *weights),
        name="experts_one",
        limit=24,
    )
    ahead_zero_peer = sent(ahead_zero, 1)
    ahead_one_peer = sent(ahead_one, 0)
    behind_one_peer = sent(behind_one, 0)
    buf_back_one = exchanged(buf_one)
    y_back_one = exchanged(after(y_one, buf_back_one))
    buf_parts_one = after(gathered_mp(combined(pick_one, buf_back_one, "combine_back_one")), y_back_one)
    y_part_one = combined(gated_one, y_back_one, "combine_one")
    y_parts_one = [y_part_one] + [
        lax.ppermute(y_part_one, "mp", [(i, (i + by) % 4) for i in range(4)]) for by in range(1, 4)
    ]
    grad_scratch = [
        pltpu.VMEM((4, TOK, 3 * SPLIT), bf16),
        pltpu.VMEM((12, TOK, TOK), bf16),
        pltpu.VMEM((16, WIDTH), f32),
    ] + weight_scratch
    back_shape = ((4 * TOK + 16, WIDTH), bf16)
    grad_sent_zero, back_one = call(
        functools.partial(backward_kernel, 1),
        [sent_shape, back_shape],
        raw=(7, 8),
        load=(1, 2, 4, 5, 6, 10, 11),
        store=(1,),
        scratch=grad_scratch,
        args=(
            ids, cotangent, state_zero, buf_parts_one, middle_one, proj_one, probs_one, w_own, w_other, gains_one,
            normed_one, context_one, gated_zero
        ),
        name="attention_back_one",
        limit=24,
    )
    back_one_peer = sent(back_one, 0)
    arrived_zero = exchanged(after(grad_sent_zero, y_part_one)).reshape(blocks)
    state_one = call(
        state_kernel,
        [token_shape],
        load=(1,),
        scratch=[pltpu.VMEM((4, TOK, WIDTH), bf16)],
        args=(ids, middle_one, *y_parts_one),
        name="state_one",
    )[0]
    arrived_zero = after(arrived_zero, ahead_zero_peer, ahead_one_peer, *y_parts_one)
    buf_zero, behind_zero = call(
        functools.partial(expert_kernel, "backward", 0),
        [(blocks, bf16), pair_shape],
        raw=(3, 4, 5, 6),
        load=(1,),
        store=(1,),
        scratch=expert_scratch,
        args=(ids, slope_zero, arrived_zero, *weights),
        name="experts_back_zero",
        limit=20,
    )
    behind_zero_peer = sent(behind_zero, 1)
    buf_back_zero = after(exchanged(buf_zero), back_one_peer, behind_one_peer)
    buf_parts_zero = gathered_mp(combined(pick_zero, buf_back_zero, "combine_back_zero"))
    back_zero = call(
        functools.partial(backward_kernel, 0),
        [back_shape],
        raw=(7, 8),
        load=(1, 2, 4, 5, 6, 10, 11),
        scratch=grad_scratch,
        args=(
            ids, back_one, inputs, buf_parts_zero, middle_zero, proj_zero, probs_zero, w_own, w_other, gains_zero,
            normed_zero, context_zero
        ),
        name="attention_back_zero",
        limit=24,
    )[0]
    back_zero_peer = sent(back_zero, 1)
    packed = call(
        weight_grad_kernel,
        [((16, 48, PACK), bf16)],
        load=(3, 4),
        args=(ids, back_zero, back_zero_peer, back_one, back_one_peer, onehot),
        name="attention_grads",
    )[0]
    shares = exchanged(packed)
    in_grad, out_grad = pl.pallas_call(
        expert_grad_kernel,
        out_shape=[jax.ShapeDtypeStruct((2, WIDTH, WIDTH), f32)] * 2,
        grid=(2,),
        in_specs=[pl.BlockSpec(memory_space=pltpu.SMEM)] + [pl.BlockSpec(memory_space=pltpu.HBM)] * 8,
        out_specs=[pl.BlockSpec((1, WIDTH, WIDTH), lambda e: (e, 0, 0))] * 2,
        scratch_shapes=[pltpu.VMEM((4, 2, 2, 256, WIDTH), bf16), pltpu.SemaphoreType.DMA((2, 4))],
        compiler_params=pltpu.CompilerParams(vmem_limit_bytes=24 * 1024 * 1024),
        name="expert_grads",
    )(
        ids,
        *map(far, (
        ahead_zero, behind_zero, ahead_zero_peer, behind_zero_peer, ahead_one, behind_one, ahead_one_peer,
        behind_one_peer
        ))
    )
    states, input_grads = call(
        assemble_kernel,
        [((2, TOK, WIDTH), bf16)] * 2,
        load=(1, 3, 4, 5, 6, 7, 8),
        args=(
            ids, state_zero, state_one, sent(state_zero, 1), sent(state_one, 0), back_zero, back_one, back_zero_peer,
            back_one_peer
        ),
        name="assemble",
    )
    qkv_grad, out_grad_part, extra = call(
        sum_kernel,
        [((3, 48, SPLIT), f32), ((48, SPLIT), f32), ((8, 48), f32)],
        scalars=0,
        args=(after(shares, in_grad, input_grads),),
        name="sum_grads",
    )
    return (
        states[None],
        input_grads[None],
        extra[0:1],
        qkv_grad.transpose(1, 0, 2)[None],
        out_grad_part[None],
        extra[2:5, 0:2].T[None],
        extra[1:2],
        in_grad[None],
        out_grad[None],
    )


def solution(mesh):
    return jax.shard_map(
        body,
        mesh=mesh,
        in_specs=(
            P(None, "dp", None),
            P(None, "dp", None),
            P(None, "dp"),
            P(),
            P("section", None, "dp", None),
            P("section", None, "dp", None),
            P("section", "dp"),
            P("section", "dp", None, "mp"),
            P("section", "dp", "mp"),
            P("section", "dp", "mp"),
            P("section", "dp"),
            P("section", "dp", None, "mp"),
            P("section", "dp", "mp", None),
        ),
        out_specs=(
            P("section", None, "dp", None),
            P("section", None, "dp", None),
            P("section", "dp"),
            P("section", "dp", None, "mp"),
            P("section", "dp", "mp"),
            P("section", "dp", "mp"),
            P("section", "dp"),
            P("section", "dp", None, "mp"),
            P("section", "dp", "mp", None),
        ),
        check_vma=False,
    )
```

```python
import functools

import jax
import jax.numpy as jnp
from jax import lax
from jax.experimental import pallas as pl
from jax.experimental.pallas import tpu as pltpu
from jax.sharding import PartitionSpec as P

bf16 = jnp.bfloat16
f32 = jnp.float32
epsilon = 1e-06
negative = -1e30
root = 0.7978845608028654
cubic = 0.044715
TOK = 128
WIDTH = 768
HEADS = 3
DH = 64
SPLIT = 192
PACK = 896
SLOTS = 512
CAP = 16


def dot(a, b):
    return lax.dot_general(a, b, (((1,), (0,)), ((), ())), preferred_element_type=f32)


def dot_nt(a, b):
    return lax.dot_general(a, b, (((1,), (1,)), ((), ())), preferred_element_type=f32)


def dot_tn(a, b):
    return lax.dot_general(a, b, (((0,), (0,)), ((), ())), preferred_element_type=f32)


def iota(shape, dim):
    return lax.broadcasted_iota(jnp.int32, shape, dim)


def norm_scale(values):
    return lax.rsqrt(jnp.mean(values * values, axis=-1, keepdims=True) + epsilon)


def swapped(x):
    return lax.ppermute(x, "section", [(0, 1), (1, 0)])


def sent(x, source):
    return lax.ppermute(x, "section", [(source, 1 - source)])


class Loaded:
    def __init__(self, source, buffer, sem):
        self.copy = pltpu.make_async_copy(source, buffer, sem)
        self.buffer, self.waiting = buffer, True
        self.copy.start()

    def ready(self):
        if self.waiting:
            self.copy.wait()
            self.waiting = False

    def __getitem__(self, index):
        self.ready()
        return self.buffer[index]


class Stored:
    def __init__(self, target, buffer, sems):
        self.target, self.buffer, self.sems, self.copies = target, buffer, sems, []
        self.dtype = target.dtype

    def __setitem__(self, index, value):
        self.buffer[index] = value

    def start(self, *index):
        source = self.buffer.at[index] if index else self.buffer
        target = self.target.at[index] if index else self.target
        copy = pltpu.make_async_copy(source, target, self.sems.at[len(self.copies)])
        copy.start()
        self.copies.append(copy)

    def finish(self):
        for copy in self.copies:
            copy.wait()


def far(x):
    return pltpu.with_memory_space_constraint(x, pltpu.HBM)


def call(kernel, outs, raw=(), load=(), store=(), scalars=1, scratch=(), args=(), name=None, limit=16):
    specs = []
    for index in range(len(args)):
        if index < scalars:
            specs.append(pl.BlockSpec(memory_space=pltpu.SMEM))
        elif index in raw or index in load:
            specs.append(pl.BlockSpec(memory_space=pltpu.HBM))
        else:
            specs.append(pl.BlockSpec(memory_space=pltpu.VMEM))
    extra = [pltpu.VMEM(args[i].shape, args[i].dtype) for i in load]
    extra += [pltpu.VMEM(*outs[i]) for i in store]
    if load:
        extra.append(pltpu.SemaphoreType.DMA((len(load),)))
    if store:
        extra.append(pltpu.SemaphoreType.DMA((len(store), 8)))

    def wrapped(*refs):
        refs = list(refs)
        count = len(args) + len(outs)
        own = refs[count : len(refs) - len(extra)]
        more = refs[len(refs) - len(extra) :]
        load_sems = more[len(load) + len(store)] if load else None
        store_sems = more[-1] if store else None
        for n, i in enumerate(load):
            refs[i] = Loaded(refs[i], more[n], load_sems.at[n])
        stored = []
        for n, i in enumerate(store):
            refs[len(args) + i] = Stored(refs[len(args) + i], more[len(load) + n], store_sems.at[n])
            stored.append(refs[len(args) + i])
        kernel(*refs[:count], *own)
        for item in refs[:count]:
            if isinstance(item, Loaded):
                item.ready()
        for item in stored:
            if not item.copies:
                item.start()
        for item in stored:
            item.finish()

    args = [far(x) if i in raw or i in load else x for i, x in enumerate(args)]
    return pl.pallas_call(
        wrapped,
        out_shape=[
            pltpu.HBM(shape, dtype) if i in store else jax.ShapeDtypeStruct(shape, dtype)
            for i, (shape, dtype) in enumerate(outs)
        ],
        in_specs=specs,
        out_specs=[
            pl.BlockSpec(memory_space=pltpu.HBM if i in store else pltpu.VMEM) for i in range(len(outs))
        ],
        scratch_shapes=list(scratch) + extra,
        compiler_params=pltpu.CompilerParams(vmem_limit_bytes=limit * 1024 * 1024),
        name=name,
    )(*args)


def fetch(here, own, other, buffer, sems):
    count = buffer.shape[0]
    lanes = pl.ds(0, WIDTH)

    @pl.when(here)
    def _():
        for i in range(count):
            pltpu.make_async_copy(own.at[i, :, lanes], buffer.at[i], sems.at[i]).start()

    @pl.when(jnp.logical_not(here))
    def _():
        for i in range(count):
            pltpu.make_async_copy(other.at[i, :, lanes], buffer.at[i], sems.at[i]).start()

    def arrived():
        for i in range(count):
            pltpu.make_async_copy(own.at[i, :, lanes], buffer.at[i], sems.at[i]).wait()

    return arrived


def pack_kernel(qkv, out_part, gain_one, gain_two, table, whole, halves):
    eye = iota((48, 48), 0) == iota((48, 48), 1)
    one = jnp.sum(jnp.where(eye, gain_one[...].astype(f32), 0.0), axis=1, keepdims=True)
    two = jnp.sum(jnp.where(eye, gain_two[...].astype(f32), 0.0), axis=1, keepdims=True)
    row, lane = iota((48, TOK), 0), iota((48, TOK), 1)
    extra = jnp.where(lane == 0, one, jnp.where(lane == 1, two, 0.0))
    values = table[...].astype(f32)
    for r in range(2):
        for h in range(HEADS):
            extra = extra + jnp.where((row == r) & (lane == 2 + h), values[r : r + 1, h : h + 1], 0.0)
    parts = [qkv[0], qkv[1], qkv[2], out_part[...]]
    line = jnp.concatenate(parts + [extra.astype(bf16), jnp.zeros((48, TOK), bf16)], axis=1)
    whole[...] = line[:, :PACK]
    halves[0] = line[:, :512]
    halves[1] = line[:, 512:]


def spread_kernel(ids, halves, received, out):
    chosen = jnp.where(ids[0] == 0, halves[0], received[...])
    for i in range(16):
        out[i] = chosen


def first_kernel(ids, inputs, own, other, onehot, mask, part_out, gains_out):
    first = ids[0] == 0
    hidden = jnp.where(first, inputs[0], inputs[1]).astype(f32)
    scaled = hidden * norm_scale(hidden)
    low = jnp.where(first, own[...], other[...])
    high = jnp.where(first, other[...], own[...])
    weight = jnp.concatenate([low, high], axis=1)
    rows = weight[:, WIDTH:PACK].astype(f32).T
    gains_out[...] = rows[0:8]
    normed = (scaled * rows[0:1]).astype(bf16)
    proj = dot(normed, weight[:, : 3 * SPLIT]).astype(bf16)
    line = dot_tn(weight[:, WIDTH:PACK], onehot[...]).astype(bf16)
    allowed = mask[...] > 0.5
    pieces = [jnp.zeros((TOK, DH), bf16)]
    for head in range(HEADS):
        probs, value = head_probs(proj, head_bias(line, allowed, head), head)
        pieces.append(dot(probs, value).astype(bf16))
    part_out[...] = dot_nt(jnp.concatenate(pieces, axis=1), weight[:, 512:WIDTH]).astype(bf16)


def dispatch_kernel(ids, inputs, parts, gain_rows, pick, middle_out, sent_out):
    hidden = jnp.where(ids[0] == 0, inputs[0], inputs[1]).astype(f32)
    for i in range(4):
        hidden = hidden + parts[i].astype(f32)
    middle_out[...] = hidden
    normed = (hidden * norm_scale(hidden) * gain_rows[1:2, :]).astype(bf16)
    sent_out[...] = dot_tn(pick[...], normed).astype(bf16)


def prepare_kernel(ids, own, other, segments, cotangent, pick_zero, pick_one, gated_zero, gated_one, mask, sent_grad):
    section = ids[0]
    first = section == 0
    row = jnp.where(first, segments[0:1, :], segments[1:2, :]).astype(f32)
    column = own[:, 0:1]
    causal = iota((TOK, TOK), 0) >= iota((TOK, TOK), 1)
    mask[...] = jnp.where(causal & (column == row), 1.0, 0.0)
    expert = iota((TOK, 32), 1).astype(f32)
    lower = jnp.where(iota((TOK, TOK), 0) > iota((TOK, TOK), 1), 1.0, 0.0).astype(bf16)
    spread = jnp.where(lax.shift_right_logical(iota((32, SLOTS), 1), 4) == iota((32, SLOTS), 0), 1.0, 0.0).astype(bf16)
    slot = iota((TOK, SLOTS), 1)
    slot_expert = lax.shift_right_logical(slot, 4).astype(f32)
    slot_place = (slot & 15).astype(f32)
    for layer in range(2):
        info = jnp.where(section == layer, own[...], other[...])
        r0, r1, g0, g1 = info[:, 1:2], info[:, 2:3], info[:, 3:4], info[:, 4:5]
        named = jnp.where((r0 == expert) | (r1 == expert), 1.0, 0.0).astype(bf16)
        earlier = dot(lower, named)
        here = dot(earlier.astype(bf16), spread) == slot_place
        d0 = here & (r0 == slot_expert)
        d1 = here & (r1 == slot_expert)
        (pick_zero, pick_one)[layer][...] = jnp.where(d0 | d1, 1.0, 0.0).astype(bf16)
        gates = jnp.where(d0, g0, jnp.where(d1, g1, 0.0)).astype(bf16)
        (gated_zero, gated_one)[layer][...] = gates
        if layer == 1:
            grad = jnp.where(first, cotangent[0], cotangent[1])
            sent_grad[...] = dot_tn(gates, grad).astype(bf16)


def head_bias(line, allowed, head):
    chosen = jnp.where(iota((TOK, TOK), 1) == 2 + head, 1.0, 0.0).astype(bf16)
    bias = pltpu.roll(dot(chosen, line), 0, 1, stride=1, stride_axis=0)
    return jnp.where(allowed, bias, negative)


def head_probs(proj, bias, head):
    at = head * DH
    query = proj[:, at : at + DH]
    key = proj[:, SPLIT + at : SPLIT + at + DH]
    value = proj[:, 2 * SPLIT + at : 2 * SPLIT + at + DH]
    scores = dot_nt(query * jnp.asarray(0.125, bf16), key) + bias
    peak = jnp.max(scores, axis=-1, keepdims=True)
    expos = jnp.exp(scores - peak)
    return (expos / jnp.sum(expos, axis=-1, keepdims=True)).astype(bf16), value


def bias_kernel(layer, ids, own, other, onehot, mask, bias_out, gains_out, extra, sem):
    lanes = pl.ds(WIDTH, TOK)

    @pl.when(ids[0] == layer)
    def _():
        pltpu.make_async_copy(own.at[:, :, lanes], extra, sem).start()

    @pl.when(ids[0] != layer)
    def _():
        pltpu.make_async_copy(other.at[:, :, lanes], extra, sem).start()

    pltpu.make_async_copy(own.at[:, :, lanes], extra, sem).wait()
    gains_out[...] = extra[0].astype(f32).T[0:8]
    allowed = mask[...] > 0.5
    for part in range(4):
        line = dot_tn(extra[part], onehot[...]).astype(bf16)
        for head in range(HEADS):
            bias_out[part * HEADS + head] = head_bias(line, allowed, head).astype(bf16)


def forward_kernel(layer, ids, *refs):
    if layer == 0:
        inputs, own, other, gain_rows, bias = refs[:5]
        rest = refs[5:]
    else:
        before, parts, own, other, gain_rows, bias, pick, state_out, sent_out, middle_out = refs[:10]
        rest = refs[10:]
    normed_out, proj_out, probs_out, context_out, contexts, weights, sems = rest
    section = ids[0]
    arrived = fetch(section == layer, own, other, weights, sems)
    if layer == 0:
        hidden = jnp.where(section == 0, inputs[0], inputs[1]).astype(f32)
    else:
        added = parts[0].astype(f32)
        for i in range(1, 4):
            added = added + parts[i].astype(f32)
        state = (before[...] + added).astype(bf16)
        state_out[...] = state
        state_out.start()
        hidden = state.astype(f32)
    normed = (hidden * norm_scale(hidden) * gain_rows[0:1, :]).astype(bf16)
    normed_out[...] = normed
    normed_out.start()
    attn = None
    arrived()
    for part in range(4):
        proj = dot(normed, weights[part, :, : 3 * SPLIT]).astype(bf16)
        proj_out[part] = proj
        proj_out.start(part)
        pieces = []
        for head in range(HEADS):
            probs, value = head_probs(proj, bias[part * HEADS + head].astype(f32), head)
            probs_out[part * HEADS + head] = probs
            pieces.append(dot(probs, value).astype(bf16))
        probs_out.start(pl.ds(part * HEADS, HEADS))
        contexts[part] = jnp.concatenate(pieces, axis=1)
        if layer == 1:
            padded = jnp.concatenate([jnp.zeros((TOK, DH), bf16)] + pieces, axis=1)
            term = dot_nt(padded, weights[part, :, 512:WIDTH])
            attn = term if attn is None else attn + term
    context_out[...] = contexts[ids[1]]
    context_out.start()
    if layer == 1:
        middle = hidden + attn
        middle_out[...] = middle
        middle_out.start()
        normed_two = (middle * norm_scale(middle) * gain_rows[1:2, :]).astype(bf16)
        sent_out[...] = dot_tn(pick[...], normed_two).astype(bf16)


def gelu_both(x):
    square = x * x
    th = jnp.tanh(root * (x + cubic * x * square))
    half = 0.5 * (1.0 + th)
    value = x * half
    slope = half + 0.5 * x * (1.0 - th * th) * (root * (1.0 + 3.0 * cubic * square))
    return value, slope


def rows_of(ref, expert):
    return ref[:, expert].reshape(256, WIDTH)


def expert_kernel(mode, layer, ids, *refs):
    if mode == "forward":
        received, in_own, in_other, out_own, out_other, y_out, ahead, slope_out = refs[:8]
    elif mode == "both":
        received, arrived_grad, in_own, in_other, out_own, out_other, y_out, buf_out, ahead, behind = refs[:10]
    else:
        slope_in, arrived_grad, in_own, in_other, out_own, out_other, buf_out, behind = refs[:8]
    w_in, w_out, in_sems, out_sems = refs[-4:]
    here = ids[0] == layer
    if mode == "backward":
        out_arrived = fetch(here, out_own, out_other, w_out, out_sems)
        in_arrived = fetch(here, in_own, in_other, w_in, in_sems)
        slopes = [slope_in[e].astype(f32) for e in range(2)]
        out_arrived()
    else:
        in_arrived = fetch(here, in_own, in_other, w_in, in_sems)
        out_arrived = fetch(here, out_own, out_other, w_out, out_sems)
        in_arrived()
        acts, slopes = [], []
        for e in range(2):
            rows = rows_of(received, e)
            value, slope = gelu_both(dot(rows, w_in[e]))
            acts.append(value.astype(bf16))
            slopes.append(slope)
            ahead[0, e] = rows
            ahead[1, e] = acts[e]
            if mode == "forward":
                slope_out[e] = slope.astype(bf16)
        ahead.start()
        if mode == "forward":
            slope_out.start()
        out_arrived()
        for e in range(2):
            y_out[:, e] = dot(acts[e], w_out[e]).astype(bf16).reshape(16, CAP, WIDTH)
    if mode != "forward":
        pres = []
        for e in range(2):
            back = rows_of(arrived_grad, e)
            pres.append((dot_nt(back, w_out[e]) * slopes[e]).astype(bf16))
            behind[0, e] = pres[e]
            behind[1, e] = back
        behind.start()
        if mode == "backward":
            in_arrived()
        for e in range(2):
            buf_out[:, e] = dot_nt(pres[e], w_in[e]).astype(bf16).reshape(16, CAP, WIDTH)


def combine_kernel(matrix, returned, out):
    out[...] = dot(matrix[...], returned[...]).astype(out.dtype)


def state_kernel(ids, before, *refs):
    parts, out, ordered = refs[:4], refs[4], refs[5]
    for by in range(4):
        ordered[(ids[1] + 4 - by) & 3] = parts[by][...]
    total = before[...]
    for i in range(4):
        total = total + ordered[i].astype(f32)
    out[...] = total.astype(bf16)


def backward_kernel(layer, ids, *refs):
    if layer == 1:
        grads, hidden_ref = refs[0], refs[1]
    else:
        grads, hidden_ref = refs[0], refs[1]
    parts, middle_ref, proj_ref, probs_ref, own, other, gain_rows, normed_ref, context_ref = refs[2:11]
    rest = refs[11:]
    if layer == 1:
        gated, rest = rest[0], rest[1:]
    if layer == 1:
        sent_out, rest = rest[0], rest[1:]
    bundle, all_proj, all_scores, small_out, weights, sems = rest
    arrived = fetch(ids[0] == layer, own, other, weights, sems)
    section = ids[0]
    device = ids[1]
    first = section == 0
    if layer == 1:
        grad = jnp.where(first, grads[0], grads[1]).astype(f32)
        hidden = hidden_ref[...].astype(f32)
    else:
        grad = grads[3 * TOK : 4 * TOK].astype(f32)
        hidden = jnp.where(first, hidden_ref[0], hidden_ref[1]).astype(f32)
    middle = middle_ref[...]
    buf = parts[0].astype(f32)
    for i in range(1, 4):
        buf = buf + parts[i].astype(f32)
    scale_two = norm_scale(middle)
    gain_one, gain_two = gain_rows[0:1, :], gain_rows[1:2, :]
    small_out[...] = jnp.zeros(small_out.shape, f32)
    unit = middle * scale_two
    small_out[1:2, :] = jnp.sum(buf * unit, axis=0, keepdims=True)
    inner = jnp.mean(unit * gain_two * buf, axis=-1, keepdims=True)
    middle_grad = grad + scale_two * (gain_two * buf - unit * inner)
    attn_low = middle_grad.astype(bf16)
    bundle[0:TOK] = normed_ref[...]
    bundle[TOK : 2 * TOK] = attn_low
    normed_grad = None
    arrived()
    for part in range(4):
        context_grad = dot(attn_low, weights[part, :, 512:WIDTH]).astype(bf16)
        proj = proj_ref[part]
        q_parts, k_parts, v_parts = [], [], []
        for head in range(HEADS):
            at = head * DH
            query = proj[:, at : at + DH]
            key = proj[:, SPLIT + at : SPLIT + at + DH]
            value = proj[:, 2 * SPLIT + at : 2 * SPLIT + at + DH]
            probs = probs_ref[part * HEADS + head]
            back = context_grad[:, DH + at : DH + at + DH]
            wide = probs.astype(f32)
            prob_grad = dot_nt(back, value)
            inner = jnp.sum(wide * prob_grad, axis=-1, keepdims=True)
            score_grad = (wide * (prob_grad - inner)).astype(bf16)
            all_scores[part * HEADS + head] = score_grad
            q_parts.append(dot(score_grad, key) * 0.125)
            k_parts.append(dot_tn(score_grad, query) * 0.125)
            v_parts.append(dot_tn(probs, back))
        proj_grad = jnp.concatenate(q_parts + k_parts + v_parts, axis=1).astype(bf16)
        all_proj[part] = proj_grad
        term = dot_nt(proj_grad, weights[part, :, : 3 * SPLIT])
        normed_grad = term if normed_grad is None else normed_grad + term
    scale_one = norm_scale(hidden)
    unit = hidden * scale_one
    small_out[0:1, :] = jnp.sum(normed_grad * unit, axis=0, keepdims=True)
    inner = jnp.mean(unit * gain_one * normed_grad, axis=-1, keepdims=True)
    low = (middle_grad + scale_one * (gain_one * normed_grad - unit * inner)).astype(bf16)
    bundle[3 * TOK : 4 * TOK] = low
    if layer == 1:
        sent_out[...] = dot_tn(gated[...], low).astype(bf16)
    bundle[2 * TOK : 3 * TOK] = jnp.concatenate([all_proj[device], context_ref[...]], axis=1)
    flip = jnp.where(iota((TOK, TOK), 0) + iota((TOK, TOK), 1) == TOK - 1, 1.0, 0.0).astype(bf16)
    for head in range(HEADS):
        flipped = dot(flip, all_scores[device * HEADS + head])
        lined = pltpu.roll(flipped, 1, 1, stride=1, stride_axis=0)
        small_out[2 + head : 3 + head, 0:TOK] = jnp.sum(lined, axis=0, keepdims=True)
    bundle[4 * TOK :] = small_out[...].astype(bf16)


def weight_grad_kernel(ids, zero, zero_peer, one, one_peer, onehot, out, buffer, sems):
    for layer in range(2):

        @pl.when(ids[0] == layer)
        def _(layer=layer):
            mine, peer = zero, zero_peer
            if layer == 1:
                copies = [pltpu.make_async_copy(x, buffer.at[i], sems.at[i]) for i, x in enumerate((one, one_peer))]
                for copy in copies:
                    copy.start()
                for copy in copies:
                    copy.wait()
                mine, peer = buffer.at[0], buffer.at[1]
            both = [jnp.concatenate([mine[i * TOK : i * TOK + TOK], peer[i * TOK : i * TOK + TOK]], axis=0) for i in range(3)]
            normed, attn, third = both
            left = dot_tn(normed, third[:, : 3 * SPLIT])
            right = dot_tn(attn, third[:, 3 * SPLIT :])
            rows = mine[4 * TOK :].astype(f32) + peer[4 * TOK :].astype(f32)
            lines = rows[:, 0:TOK].astype(bf16)
            keep = (iota((TOK, 16), 1) >= 2) & (iota((TOK, 16), 1) < 5) & (iota((TOK, 16), 0) == iota((TOK, 16), 1))
            lines = dot(jnp.where(keep, 1.0, 0.0).astype(bf16), lines).astype(bf16)
            table = dot_nt(onehot[...], lines)
            tall = jnp.concatenate([rows, jnp.zeros((TOK - 16, WIDTH), f32)], axis=0).T
            lane = iota((WIDTH, TOK), 1)
            extra = jnp.where(lane < 2, tall, table)
            out[...] = jnp.concatenate([left, right, extra], axis=1).astype(bf16).reshape(16, 48, PACK)


def sum_kernel(received, qkv, out_part, gain_one, gain_two, table):
    total = received[0].astype(f32)
    for i in range(1, 16):
        total = total + received[i].astype(f32)
    for c in range(3):
        qkv[c] = total[:, c * SPLIT : (c + 1) * SPLIT]
    out_part[...] = total[:, 3 * SPLIT : WIDTH]
    rows = total[:, WIDTH:].T
    gain_one[...] = rows[0:1, :]
    gain_two[...] = rows[1:2, :]
    table[...] = total[0:2, WIDTH + 2 : WIDTH + 5]


def assemble_kernel(ids, state_zero, state_one, state_zero_peer, state_one_peer, zero, one, zero_peer, one_peer, states, grads):
    rows = slice(3 * TOK, 4 * TOK)
    for item in (state_zero, state_zero_peer, state_one_peer, zero, one, zero_peer, one_peer):
        item.ready()

    @pl.when(ids[0] == 0)
    def _():
        states[0] = state_zero[...]
        states[1] = state_zero_peer[...]
        grads[0] = zero[rows]
        grads[1] = zero_peer[rows]

    @pl.when(ids[0] == 1)
    def _():
        states[0] = state_one_peer[...]
        states[1] = state_one[...]
        grads[0] = one_peer[rows]
        grads[1] = one[rows]


def expert_grad_kernel(ids, *refs):
    layers = (refs[0:4], refs[4:8])
    in_out, out_out, buffer, sems = refs[8:]
    expert = pl.program_id(0)

    @pl.when(expert == 0)
    def _():
        for layer, sources in enumerate(layers):

            @pl.when(ids[0] == layer)
            def _(sources=sources):
                for e in range(2):
                    for i, source in enumerate(sources):
                        pltpu.make_async_copy(source.at[:, e], buffer.at[i, :, e], sems.at[e, i]).start()

    for e in range(2):

        @pl.when(expert == e)
        def _(e=e):
            for i, source in enumerate(layers[0]):
                pltpu.make_async_copy(source.at[:, e], buffer.at[i, :, e], sems.at[e, i]).wait()

    rows, act = [jnp.concatenate([buffer[0, i, expert], buffer[2, i, expert]], axis=0) for i in range(2)]
    pre, back = [jnp.concatenate([buffer[1, i, expert], buffer[3, i, expert]], axis=0) for i in range(2)]
    in_out[0] = dot_tn(rows, pre)
    out_out[0] = dot_tn(act, back)


def after(x, *earlier):
    return lax.optimization_barrier((x, *earlier))[0]


def exchanged(x):
    return lax.all_to_all(x.reshape(16, -1, x.shape[-1]), "dp", 0, 0, tiled=True)


def gathered_mp(x):
    return lax.all_gather(x, "mp", axis=0)


def body(
    inputs, cotangent, segments, buckets, routes, gates, attn_gain, qkv_weight, out_weight, rel_bias, ffn_gain, w_in, w_out
):
    section = lax.axis_index("section")
    ids = jnp.stack([section, lax.axis_index("mp")]).astype(jnp.int32)
    pack, halves = call(
        pack_kernel,
        [((48, PACK), bf16), ((2, 48, 512), bf16)],
        scalars=0,
        load=(0, 1, 2, 3, 4),
        args=(qkv_weight[0].transpose(1, 0, 2), out_weight[0], attn_gain, ffn_gain, rel_bias[0]),
        name="pack",
    )
    spread = call(
        spread_kernel, [((16, 48, 512), bf16)], args=(ids, halves, sent(halves[1], 0)), name="spread"
    )[0]
    w_own = lax.all_gather(pack, ("mp", "dp"), axis=0).reshape(4, WIDTH, PACK)
    in_own, out_own = w_in[0], w_out[0]
    in_other, out_other = swapped(after(in_own, spread)), swapped(after(out_own, spread))
    info = jnp.concatenate(
        [segments.astype(f32)[:, :, None], routes[0].astype(f32), gates[0], jnp.zeros((2, TOK, 3), f32)], axis=2
    )
    info_own = lax.dynamic_index_in_dim(info, section, 0, False)
    info_other = swapped(lax.dynamic_index_in_dim(info, 1 - section, 0, False))
    reverse = jnp.concatenate([buckets[0:1], buckets[1:][::-1]])
    place = jnp.arange(WIDTH, dtype=jnp.int32)
    number = jnp.where(place % 48 < 2, 2 * (place // 48) + place % 48, -1)
    onehot = (number[:, None] == reverse[None, :]).astype(bf16)

    choice = ((TOK, SLOTS), bf16)
    token_shape = ((TOK, WIDTH), bf16)
    sent_shape = ((SLOTS, WIDTH), bf16)
    middle_shape = ((TOK, WIDTH), f32)
    gain_shape = ((8, WIDTH), f32)
    pick_zero, pick_one, gated_zero, gated_one, mask, grad_sent = call(
        prepare_kernel,
        [choice, choice, choice, choice, ((TOK, TOK), f32), sent_shape],
        load=(4,),
        args=(ids, info_own, info_other, segments, cotangent),
        name="prepare",
    )
    half_own = after(exchanged(spread).reshape(WIDTH, 512), mask)
    half_other = swapped(half_own)
    blocks = (16, 2, CAP, WIDTH)
    arrived_one = exchanged(grad_sent).reshape(blocks)
    part_zero, gains_zero = call(
        first_kernel,
        [token_shape, gain_shape],
        load=(1,),
        args=(ids, inputs, half_own, half_other, onehot, mask),
        name="first",
    )
    middle_zero, sent_zero = call(
        dispatch_kernel,
        [middle_shape, sent_shape],
        load=(1,),
        store=(0,),
        args=(ids, inputs, after(gathered_mp(part_zero), arrived_one), gains_zero, pick_zero),
        name="dispatch_zero",
    )
    pair_shape = ((2, 2, 256, WIDTH), bf16)
    received_zero = exchanged(sent_zero).reshape(blocks)
    weights = (in_own, in_other, out_own, out_other)
    expert_scratch = [
        pltpu.VMEM((2, WIDTH, WIDTH), bf16),
        pltpu.VMEM((2, WIDTH, WIDTH), bf16),
        pltpu.SemaphoreType.DMA((2,)),
        pltpu.SemaphoreType.DMA((2,)),
    ]
    y_zero, ahead_zero, slope_zero = call(
        functools.partial(expert_kernel, "forward", 0),
        [(blocks, bf16), pair_shape, ((2, 256, WIDTH), bf16)],
        raw=(2, 3, 4, 5),
        store=(1, 2),
        scratch=expert_scratch,
        args=(ids, received_zero, *weights),
        name="experts_zero",
        limit=20,
    )
    w_own = after(w_own, y_zero)
    w_other = swapped(w_own)

    def combined(matrix, back, name):
        return call(
            combine_kernel, [token_shape], scalars=0, args=(matrix, back.reshape(SLOTS, WIDTH)), name=name
        )[0]

    bias_shape = ((12, TOK, TOK), bf16)
    bias_scratch = [pltpu.VMEM((4, WIDTH, TOK), bf16), pltpu.SemaphoreType.DMA]

    def biased(layer, name):
        return call(
            functools.partial(bias_kernel, layer),
            [bias_shape, gain_shape],
            raw=(1, 2),
            store=(0,),
            scratch=bias_scratch,
            args=(ids, w_own, w_other, onehot, mask),
            name=name,
        )

    bias_one, gains_one = biased(1, "bias_one")
    y_back_zero = after(exchanged(y_zero), gains_one)
    parts_zero = gathered_mp(combined(gated_zero, y_back_zero, "combine_zero"))
    kept_shapes = [token_shape, ((4, TOK, 3 * SPLIT), bf16), bias_shape, ((TOK, SPLIT), bf16)]
    weight_scratch = [pltpu.VMEM((4, WIDTH, WIDTH), bf16), pltpu.SemaphoreType.DMA((4,))]
    forward_scratch = [pltpu.VMEM((4, TOK, SPLIT), bf16)] + weight_scratch
    state_zero, sent_one, middle_one, normed_one, proj_one, probs_one, context_one = call(
        functools.partial(forward_kernel, 1),
        [token_shape, sent_shape, middle_shape] + kept_shapes,
        raw=(3, 4),
        load=(1, 6),
        store=(0, 2, 3, 4, 5, 6),
        scratch=forward_scratch,
        args=(ids, middle_zero, parts_zero, w_own, w_other, gains_one, bias_one, pick_one),
        name="attention_one",
        limit=20,
    )
    bias_zero = biased(0, "bias_zero")[0]
    normed_zero, proj_zero, probs_zero, context_zero = call(
        functools.partial(forward_kernel, 0),
        kept_shapes,
        raw=(2, 3),
        load=(1, 5),
        store=(0, 1, 2, 3),
        scratch=forward_scratch,
        args=(ids, inputs, w_own, after(w_other, sent_one), gains_zero, bias_zero),
        name="attention_zero",
        limit=20,
    )
    received_one = after(exchanged(sent_one).reshape(blocks), normed_zero)
    y_one, buf_one, ahead_one, behind_one = call(
        functools.partial(expert_kernel, "both", 1),
        [(blocks, bf16), (blocks, bf16), pair_shape, pair_shape],
        raw=(3, 4, 5, 6),
        store=(2, 3),
        scratch=expert_scratch,
        args=(ids, received_one, arrived_one, *weights),
        name="experts_one",
        limit=24,
    )
    ahead_zero_peer = sent(ahead_zero, 1)
    ahead_one_peer = sent(ahead_one, 0)
    behind_one_peer = sent(behind_one, 0)
    buf_back_one = exchanged(buf_one)
    y_back_one = exchanged(after(y_one, buf_back_one))
    buf_parts_one = after(gathered_mp(combined(pick_one, buf_back_one, "combine_back_one")), y_back_one)
    y_part_one = combined(gated_one, y_back_one, "combine_one")
    y_parts_one = [y_part_one] + [
        lax.ppermute(y_part_one, "mp", [(i, (i + by) % 4) for i in range(4)]) for by in range(1, 4)
    ]
    grad_scratch = [
        pltpu.VMEM((4, TOK, 3 * SPLIT), bf16),
        pltpu.VMEM((12, TOK, TOK), bf16),
        pltpu.VMEM((16, WIDTH), f32),
    ] + weight_scratch
    back_shape = ((4 * TOK + 16, WIDTH), bf16)
    grad_sent_zero, back_one = call(
        functools.partial(backward_kernel, 1),
        [sent_shape, back_shape],
        raw=(7, 8),
        load=(1, 2, 4, 5, 6, 10, 11),
        store=(1,),
        scratch=grad_scratch,
        args=(
            ids, cotangent, state_zero, buf_parts_one, middle_one, proj_one, probs_one, w_own, w_other, gains_one,
            normed_one, context_one, gated_zero
        ),
        name="attention_back_one",
        limit=24,
    )
    back_one_peer = sent(back_one, 0)
    arrived_zero = exchanged(after(grad_sent_zero, y_part_one)).reshape(blocks)
    state_one = call(
        state_kernel,
        [token_shape],
        load=(1,),
        scratch=[pltpu.VMEM((4, TOK, WIDTH), bf16)],
        args=(ids, middle_one, *y_parts_one),
        name="state_one",
    )[0]
    arrived_zero = after(arrived_zero, ahead_zero_peer, ahead_one_peer, behind_one_peer, *y_parts_one)
    buf_zero, behind_zero = call(
        functools.partial(expert_kernel, "backward", 0),
        [(blocks, bf16), pair_shape],
        raw=(3, 4, 5, 6),
        load=(1,),
        store=(1,),
        scratch=expert_scratch,
        args=(ids, slope_zero, arrived_zero, *weights),
        name="experts_back_zero",
        limit=20,
    )
    buf_back_zero = after(exchanged(buf_zero), back_one_peer)
    buf_parts_zero = gathered_mp(combined(pick_zero, buf_back_zero, "combine_back_zero"))
    back_zero = call(
        functools.partial(backward_kernel, 0),
        [back_shape],
        raw=(7, 8),
        load=(1, 2, 4, 5, 6, 10, 11),
        scratch=grad_scratch,
        args=(
            ids, back_one, inputs, buf_parts_zero, middle_zero, proj_zero, probs_zero, w_own, w_other, gains_zero,
            normed_zero, context_zero
        ),
        name="attention_back_zero",
        limit=24,
    )[0]
    back_zero_peer = sent(back_zero, 1)
    packed = call(
        weight_grad_kernel,
        [((16, 48, PACK), bf16)],
        raw=(3, 4),
        scratch=[pltpu.VMEM((2,) + back_shape[0], bf16), pltpu.SemaphoreType.DMA((2,))],
        args=(ids, back_zero, back_zero_peer, back_one, back_one_peer, onehot),
        name="attention_grads",
    )[0]
    shares = exchanged(packed)
    behind_zero_peer = sent(after(behind_zero, packed), 1)
    in_grad, out_grad = pl.pallas_call(
        expert_grad_kernel,
        out_shape=[jax.ShapeDtypeStruct((2, WIDTH, WIDTH), f32)] * 2,
        grid=(2,),
        in_specs=[pl.BlockSpec(memory_space=pltpu.SMEM)] + [pl.BlockSpec(memory_space=pltpu.HBM)] * 8,
        out_specs=[pl.BlockSpec((1, WIDTH, WIDTH), lambda e: (e, 0, 0))] * 2,
        scratch_shapes=[pltpu.VMEM((4, 2, 2, 256, WIDTH), bf16), pltpu.SemaphoreType.DMA((2, 4))],
        compiler_params=pltpu.CompilerParams(vmem_limit_bytes=24 * 1024 * 1024),
        name="expert_grads",
    )(
        ids,
        *map(far, (
        ahead_zero, behind_zero, ahead_zero_peer, behind_zero_peer, ahead_one, behind_one, ahead_one_peer,
        behind_one_peer
        ))
    )
    states, input_grads = call(
        assemble_kernel,
        [((2, TOK, WIDTH), bf16)] * 2,
        load=(1, 3, 4, 5, 6, 7, 8),
        args=(
            ids, state_zero, state_one, sent(state_zero, 1), sent(state_one, 0), back_zero, back_one, back_zero_peer,
            back_one_peer
        ),
        name="assemble",
    )
    qkv_grad, out_grad_part, gain_one_grad, gain_two_grad, table_grad = call(
        sum_kernel,
        [((3, 48, SPLIT), f32), ((48, SPLIT), f32), ((1, 48), f32), ((1, 48), f32), ((2, 3), f32)],
        scalars=0,
        args=(after(shares, in_grad, input_grads),),
        name="sum_grads",
    )
    return (
        states[None],
        input_grads[None],
        gain_one_grad,
        qkv_grad.transpose(1, 0, 2)[None],
        out_grad_part[None],
        table_grad[None],
        gain_two_grad,
        in_grad[None],
        out_grad[None],
    )


def solution(mesh):
    return jax.shard_map(
        body,
        mesh=mesh,
        in_specs=(
            P(None, "dp", None),
            P(None, "dp", None),
            P(None, "dp"),
            P(),
            P("section", None, "dp", None),
            P("section", None, "dp", None),
            P("section", "dp"),
            P("section", "dp", None, "mp"),
            P("section", "dp", "mp"),
            P("section", "dp", "mp"),
            P("section", "dp"),
            P("section", "dp", None, "mp"),
            P("section", "dp", "mp", None),
        ),
        out_specs=(
            P("section", None, "dp", None),
            P("section", None, "dp", None),
            P("section", "dp"),
            P("section", "dp", None, "mp"),
            P("section", "dp", "mp"),
            P("section", "dp", "mp"),
            P("section", "dp"),
            P("section", "dp", None, "mp"),
            P("section", "dp", "mp", None),
        ),
        check_vma=False,
    )
```

```python
import functools

import jax
import jax.numpy as jnp
from jax import lax
from jax.experimental import pallas as pl
from jax.experimental.pallas import tpu as pltpu
from jax.sharding import PartitionSpec as P

bf16 = jnp.bfloat16
f32 = jnp.float32
epsilon = 1e-06
negative = -1e30
root = 0.7978845608028654
cubic = 0.044715
TOK = 128
WIDTH = 768
HEADS = 3
DH = 64
SPLIT = 192
PACK = 896
SLOTS = 512
CAP = 16


def dot(a, b):
    return lax.dot_general(a, b, (((1,), (0,)), ((), ())), preferred_element_type=f32)


def dot_nt(a, b):
    return lax.dot_general(a, b, (((1,), (1,)), ((), ())), preferred_element_type=f32)


def dot_tn(a, b):
    return lax.dot_general(a, b, (((0,), (0,)), ((), ())), preferred_element_type=f32)


def iota(shape, dim):
    return lax.broadcasted_iota(jnp.int32, shape, dim)


def norm_scale(values):
    return lax.rsqrt(jnp.mean(values * values, axis=-1, keepdims=True) + epsilon)


def swapped(x):
    return lax.ppermute(x, "section", [(0, 1), (1, 0)])


def sent(x, source):
    return lax.ppermute(x, "section", [(source, 1 - source)])


class Loaded:
    def __init__(self, source, buffer, sem):
        self.copy = pltpu.make_async_copy(source, buffer, sem)
        self.buffer, self.waiting = buffer, True
        self.copy.start()

    def ready(self):
        if self.waiting:
            self.copy.wait()
            self.waiting = False

    def __getitem__(self, index):
        self.ready()
        return self.buffer[index]


class Stored:
    def __init__(self, target, buffer, sems):
        self.target, self.buffer, self.sems, self.copies = target, buffer, sems, []
        self.dtype = target.dtype

    def __setitem__(self, index, value):
        self.buffer[index] = value

    def start(self, *index):
        source = self.buffer.at[index] if index else self.buffer
        target = self.target.at[index] if index else self.target
        copy = pltpu.make_async_copy(source, target, self.sems.at[len(self.copies)])
        copy.start()
        self.copies.append(copy)

    def finish(self):
        for copy in self.copies:
            copy.wait()


def far(x):
    return pltpu.with_memory_space_constraint(x, pltpu.HBM)


def call(kernel, outs, raw=(), load=(), store=(), scalars=1, scratch=(), args=(), name=None, limit=16):
    specs = []
    for index in range(len(args)):
        if index < scalars:
            specs.append(pl.BlockSpec(memory_space=pltpu.SMEM))
        elif index in raw or index in load:
            specs.append(pl.BlockSpec(memory_space=pltpu.HBM))
        else:
            specs.append(pl.BlockSpec(memory_space=pltpu.VMEM))
    extra = [pltpu.VMEM(args[i].shape, args[i].dtype) for i in load]
    extra += [pltpu.VMEM(*outs[i]) for i in store]
    if load:
        extra.append(pltpu.SemaphoreType.DMA((len(load),)))
    if store:
        extra.append(pltpu.SemaphoreType.DMA((len(store), 8)))

    def wrapped(*refs):
        refs = list(refs)
        count = len(args) + len(outs)
        own = refs[count : len(refs) - len(extra)]
        more = refs[len(refs) - len(extra) :]
        load_sems = more[len(load) + len(store)] if load else None
        store_sems = more[-1] if store else None
        for n, i in enumerate(load):
            refs[i] = Loaded(refs[i], more[n], load_sems.at[n])
        stored = []
        for n, i in enumerate(store):
            refs[len(args) + i] = Stored(refs[len(args) + i], more[len(load) + n], store_sems.at[n])
            stored.append(refs[len(args) + i])
        kernel(*refs[:count], *own)
        for item in refs[:count]:
            if isinstance(item, Loaded):
                item.ready()
        for item in stored:
            if not item.copies:
                item.start()
        for item in stored:
            item.finish()

    args = [far(x) if i in raw or i in load else x for i, x in enumerate(args)]
    return pl.pallas_call(
        wrapped,
        out_shape=[
            pltpu.HBM(shape, dtype) if i in store else jax.ShapeDtypeStruct(shape, dtype)
            for i, (shape, dtype) in enumerate(outs)
        ],
        in_specs=specs,
        out_specs=[
            pl.BlockSpec(memory_space=pltpu.HBM if i in store else pltpu.VMEM) for i in range(len(outs))
        ],
        scratch_shapes=list(scratch) + extra,
        compiler_params=pltpu.CompilerParams(vmem_limit_bytes=limit * 1024 * 1024),
        name=name,
    )(*args)


def fetch(here, own, other, buffer, sems):
    count = buffer.shape[0]
    lanes = pl.ds(0, WIDTH)

    @pl.when(here)
    def _():
        for i in range(count):
            pltpu.make_async_copy(own.at[i, :, lanes], buffer.at[i], sems.at[i]).start()

    @pl.when(jnp.logical_not(here))
    def _():
        for i in range(count):
            pltpu.make_async_copy(other.at[i, :, lanes], buffer.at[i], sems.at[i]).start()

    def arrived(start=0, stop=count):
        for i in range(start, stop):
            pltpu.make_async_copy(own.at[i, :, lanes], buffer.at[i], sems.at[i]).wait()

    return arrived


def pack_kernel(qkv, out_part, gain_one, gain_two, table, whole, halves):
    eye = iota((48, 48), 0) == iota((48, 48), 1)
    one = jnp.sum(jnp.where(eye, gain_one[...].astype(f32), 0.0), axis=1, keepdims=True)
    two = jnp.sum(jnp.where(eye, gain_two[...].astype(f32), 0.0), axis=1, keepdims=True)
    row, lane = iota((48, TOK), 0), iota((48, TOK), 1)
    extra = jnp.where(lane == 0, one, jnp.where(lane == 1, two, 0.0))
    values = table[...].astype(f32)
    for r in range(2):
        for h in range(HEADS):
            extra = extra + jnp.where((row == r) & (lane == 2 + h), values[r : r + 1, h : h + 1], 0.0)
    parts = [qkv[0], qkv[1], qkv[2], out_part[...]]
    line = jnp.concatenate(parts + [extra.astype(bf16), jnp.zeros((48, TOK), bf16)], axis=1)
    whole[...] = line[:, :PACK]
    halves[0] = line[:, :512]
    halves[1] = line[:, 512:]


def spread_kernel(ids, halves, received, out):
    chosen = jnp.where(ids[0] == 0, halves[0], received[...])
    for i in range(16):
        out[i] = chosen


def first_kernel(ids, inputs, own, other, onehot, mask, part_out, gains_out):
    first = ids[0] == 0
    hidden = jnp.where(first, inputs[0], inputs[1]).astype(f32)
    scaled = hidden * norm_scale(hidden)
    low = jnp.where(first, own[...], other[...])
    high = jnp.where(first, other[...], own[...])
    weight = jnp.concatenate([low, high], axis=1)
    rows = weight[:, WIDTH:PACK].astype(f32).T
    gains_out[...] = rows[0:8]
    normed = (scaled * rows[0:1]).astype(bf16)
    proj = dot(normed, weight[:, : 3 * SPLIT]).astype(bf16)
    line = dot_tn(weight[:, WIDTH:PACK], onehot[...]).astype(bf16)
    allowed = mask[...] > 0.5
    pieces = [jnp.zeros((TOK, DH), bf16)]
    for head in range(HEADS):
        probs, value = head_probs(proj, head_bias(line, allowed, head), head)
        pieces.append(dot(probs, value).astype(bf16))
    part_out[...] = dot_nt(jnp.concatenate(pieces, axis=1), weight[:, 512:WIDTH]).astype(bf16)


def dispatch_kernel(ids, inputs, parts, gain_rows, pick, middle_out, sent_out):
    hidden = jnp.where(ids[0] == 0, inputs[0], inputs[1]).astype(f32)
    for i in range(4):
        hidden = hidden + parts[i].astype(f32)
    middle_out[...] = hidden
    normed = (hidden * norm_scale(hidden) * gain_rows[1:2, :]).astype(bf16)
    sent_out[...] = dot_tn(pick[...], normed).astype(bf16)


def prepare_kernel(ids, own, other, segments, cotangent, pick_zero, pick_one, gated_zero, gated_one, mask, sent_grad):
    section = ids[0]
    first = section == 0
    row = jnp.where(first, segments[0:1, :], segments[1:2, :]).astype(f32)
    column = own[:, 0:1]
    causal = iota((TOK, TOK), 0) >= iota((TOK, TOK), 1)
    mask[...] = jnp.where(causal & (column == row), 1.0, 0.0)
    expert = iota((TOK, 32), 1).astype(f32)
    lower = jnp.where(iota((TOK, TOK), 0) > iota((TOK, TOK), 1), 1.0, 0.0).astype(bf16)
    spread = jnp.where(lax.shift_right_logical(iota((32, SLOTS), 1), 4) == iota((32, SLOTS), 0), 1.0, 0.0).astype(bf16)
    slot = iota((TOK, SLOTS), 1)
    slot_expert = lax.shift_right_logical(slot, 4).astype(f32)
    slot_place = (slot & 15).astype(f32)
    for layer in range(2):
        info = jnp.where(section == layer, own[...], other[...])
        r0, r1, g0, g1 = info[:, 1:2], info[:, 2:3], info[:, 3:4], info[:, 4:5]
        named = jnp.where((r0 == expert) | (r1 == expert), 1.0, 0.0).astype(bf16)
        earlier = dot(lower, named)
        here = dot(earlier.astype(bf16), spread) == slot_place
        d0 = here & (r0 == slot_expert)
        d1 = here & (r1 == slot_expert)
        (pick_zero, pick_one)[layer][...] = jnp.where(d0 | d1, 1.0, 0.0).astype(bf16)
        gates = jnp.where(d0, g0, jnp.where(d1, g1, 0.0)).astype(bf16)
        (gated_zero, gated_one)[layer][...] = gates
        if layer == 1:
            grad = jnp.where(first, cotangent[0], cotangent[1])
            sent_grad[...] = dot_tn(gates, grad).astype(bf16)


def head_bias(line, allowed, head):
    chosen = jnp.where(iota((TOK, TOK), 1) == 2 + head, 1.0, 0.0).astype(bf16)
    bias = pltpu.roll(dot(chosen, line), 0, 1, stride=1, stride_axis=0)
    return jnp.where(allowed, bias, negative)


def head_probs(proj, bias, head):
    at = head * DH
    query = proj[:, at : at + DH]
    key = proj[:, SPLIT + at : SPLIT + at + DH]
    value = proj[:, 2 * SPLIT + at : 2 * SPLIT + at + DH]
    scores = dot_nt(query * jnp.asarray(0.125, bf16), key) + bias
    peak = jnp.max(scores, axis=-1, keepdims=True)
    expos = jnp.exp(scores - peak)
    return (expos / jnp.sum(expos, axis=-1, keepdims=True)).astype(bf16), value


def bias_kernel(layer, ids, own, other, onehot, mask, bias_out, gains_out, extra, sem):
    lanes = pl.ds(WIDTH, TOK)

    @pl.when(ids[0] == layer)
    def _():
        pltpu.make_async_copy(own.at[:, :, lanes], extra, sem).start()

    @pl.when(ids[0] != layer)
    def _():
        pltpu.make_async_copy(other.at[:, :, lanes], extra, sem).start()

    pltpu.make_async_copy(own.at[:, :, lanes], extra, sem).wait()
    gains_out[...] = extra[0].astype(f32).T[0:8]
    allowed = mask[...] > 0.5
    for part in range(4):
        line = dot_tn(extra[part], onehot[...]).astype(bf16)
        for head in range(HEADS):
            bias_out[part * HEADS + head] = head_bias(line, allowed, head).astype(bf16)


def forward_kernel(layer, ids, *refs):
    if layer == 0:
        inputs, own, other, gain_rows, bias = refs[:5]
        rest = refs[5:]
    else:
        before, parts, own, other, gain_rows, bias, pick, state_out, sent_out, middle_out = refs[:10]
        rest = refs[10:]
    normed_out, proj_out, probs_out, context_out, contexts, weights, sems = rest
    section = ids[0]
    arrived = fetch(section == layer, own, other, weights, sems)
    if layer == 0:
        hidden = jnp.where(section == 0, inputs[0], inputs[1]).astype(f32)
    else:
        added = parts[0].astype(f32)
        for i in range(1, 4):
            added = added + parts[i].astype(f32)
        state = (before[...] + added).astype(bf16)
        state_out[...] = state
        state_out.start()
        hidden = state.astype(f32)
    normed = (hidden * norm_scale(hidden) * gain_rows[0:1, :]).astype(bf16)
    normed_out[...] = normed
    normed_out.start()
    attn = None
    for part in range(4):
        if part % 2 == 0:
            arrived(part, part + 2)
        proj = dot(normed, weights[part, :, : 3 * SPLIT]).astype(bf16)
        proj_out[part] = proj
        proj_out.start(part)
        pieces = []
        for head in range(HEADS):
            probs, value = head_probs(proj, bias[part * HEADS + head].astype(f32), head)
            probs_out[part * HEADS + head] = probs
            pieces.append(dot(probs, value).astype(bf16))
        probs_out.start(pl.ds(part * HEADS, HEADS))
        contexts[part] = jnp.concatenate(pieces, axis=1)
        if layer == 1:
            padded = jnp.concatenate([jnp.zeros((TOK, DH), bf16)] + pieces, axis=1)
            term = dot_nt(padded, weights[part, :, 512:WIDTH])
            attn = term if attn is None else attn + term
    context_out[...] = contexts[ids[1]]
    context_out.start()
    if layer == 1:
        middle = hidden + attn
        middle_out[...] = middle
        middle_out.start()
        normed_two = (middle * norm_scale(middle) * gain_rows[1:2, :]).astype(bf16)
        sent_out[...] = dot_tn(pick[...], normed_two).astype(bf16)


def gelu_both(x):
    square = x * x
    th = jnp.tanh(root * (x + cubic * x * square))
    half = 0.5 * (1.0 + th)
    value = x * half
    slope = half + 0.5 * x * (1.0 - th * th) * (root * (1.0 + 3.0 * cubic * square))
    return value, slope


def rows_of(ref, expert):
    return ref[:, expert].reshape(256, WIDTH)


def expert_kernel(mode, layer, ids, *refs):
    if mode == "forward":
        received, in_own, in_other, out_own, out_other, y_out, ahead, slope_out = refs[:8]
    elif mode == "both":
        received, arrived_grad, in_own, in_other, out_own, out_other, y_out, buf_out, ahead, behind = refs[:10]
    else:
        slope_in, arrived_grad, in_own, in_other, out_own, out_other, buf_out, behind = refs[:8]
    w_in, w_out, in_sems, out_sems = refs[-4:]
    here = ids[0] == layer
    if mode != "forward":
        backs = [rows_of(arrived_grad, e) for e in range(2)]
    if mode == "backward":
        out_arrived = fetch(here, out_own, out_other, w_out, out_sems)
        in_arrived = fetch(here, in_own, in_other, w_in, in_sems)
        slopes = [slope_in[e].astype(f32) for e in range(2)]
        for e in range(2):
            behind[1, e] = backs[e]
        behind.start(1)
        out_arrived()
    else:
        in_arrived = fetch(here, in_own, in_other, w_in, in_sems)
        out_arrived = fetch(here, out_own, out_other, w_out, out_sems)
        acts, slopes = [], []
        for e in range(2):
            ahead[0, e] = rows_of(received, e)
        ahead.start(0)
        if mode == "both":
            for e in range(2):
                behind[1, e] = backs[e]
            behind.start(1)
        in_arrived()
        for e in range(2):
            rows = rows_of(received, e)
            value, slope = gelu_both(dot(rows, w_in[e]))
            acts.append(value.astype(bf16))
            slopes.append(slope)
            ahead[1, e] = acts[e]
            if mode == "forward":
                slope_out[e] = slope.astype(bf16)
        ahead.start(1)
        if mode == "forward":
            slope_out.start()
        out_arrived()
        for e in range(2):
            y_out[:, e] = dot(acts[e], w_out[e]).astype(bf16).reshape(16, CAP, WIDTH)
    if mode != "forward":
        pres = []
        for e in range(2):
            pres.append((dot_nt(backs[e], w_out[e]) * slopes[e]).astype(bf16))
            behind[0, e] = pres[e]
        behind.start(0)
        if mode == "backward":
            in_arrived()
        for e in range(2):
            buf_out[:, e] = dot_nt(pres[e], w_in[e]).astype(bf16).reshape(16, CAP, WIDTH)


def combine_kernel(matrix, returned, out):
    out[...] = dot(matrix[...], returned[...]).astype(out.dtype)


def state_kernel(ids, before, *refs):
    parts, out, ordered = refs[:4], refs[4], refs[5]
    for by in range(4):
        ordered[(ids[1] + 4 - by) & 3] = parts[by][...]
    total = before[...]
    for i in range(4):
        total = total + ordered[i].astype(f32)
    out[...] = total.astype(bf16)


def backward_kernel(layer, ids, *refs):
    if layer == 1:
        grads, hidden_ref = refs[0], refs[1]
    else:
        grads, hidden_ref = refs[0], refs[1]
    parts, middle_ref, proj_ref, probs_ref, own, other, gain_rows, normed_ref, context_ref = refs[2:11]
    rest = refs[11:]
    if layer == 1:
        gated, rest = rest[0], rest[1:]
    if layer == 1:
        sent_out, rest = rest[0], rest[1:]
    bundle, all_proj, all_scores, small_out, weights, sems = rest
    arrived = fetch(ids[0] == layer, own, other, weights, sems)
    section = ids[0]
    device = ids[1]
    first = section == 0
    if layer == 1:
        grad = jnp.where(first, grads[0], grads[1]).astype(f32)
        hidden = hidden_ref[...].astype(f32)
    else:
        grad = grads[3 * TOK : 4 * TOK].astype(f32)
        hidden = jnp.where(first, hidden_ref[0], hidden_ref[1]).astype(f32)
    middle = middle_ref[...]
    buf = parts[0].astype(f32)
    for i in range(1, 4):
        buf = buf + parts[i].astype(f32)
    scale_two = norm_scale(middle)
    gain_one, gain_two = gain_rows[0:1, :], gain_rows[1:2, :]
    small_out[...] = jnp.zeros(small_out.shape, f32)
    unit = middle * scale_two
    small_out[1:2, :] = jnp.sum(buf * unit, axis=0, keepdims=True)
    inner = jnp.mean(unit * gain_two * buf, axis=-1, keepdims=True)
    middle_grad = grad + scale_two * (gain_two * buf - unit * inner)
    attn_low = middle_grad.astype(bf16)
    bundle[0:TOK] = normed_ref[...]
    bundle[TOK : 2 * TOK] = attn_low
    normed_grad = None
    for part in range(4):
        if part % 2 == 0:
            arrived(part, part + 2)
        context_grad = dot(attn_low, weights[part, :, 512:WIDTH]).astype(bf16)
        proj = proj_ref[part]
        q_parts, k_parts, v_parts = [], [], []
        for head in range(HEADS):
            at = head * DH
            query = proj[:, at : at + DH]
            key = proj[:, SPLIT + at : SPLIT + at + DH]
            value = proj[:, 2 * SPLIT + at : 2 * SPLIT + at + DH]
            probs = probs_ref[part * HEADS + head]
            back = context_grad[:, DH + at : DH + at + DH]
            wide = probs.astype(f32)
            prob_grad = dot_nt(back, value)
            inner = jnp.sum(wide * prob_grad, axis=-1, keepdims=True)
            score_grad = (wide * (prob_grad - inner)).astype(bf16)
            all_scores[part * HEADS + head] = score_grad
            q_parts.append(dot(score_grad, key) * 0.125)
            k_parts.append(dot_tn(score_grad, query) * 0.125)
            v_parts.append(dot_tn(probs, back))
        proj_grad = jnp.concatenate(q_parts + k_parts + v_parts, axis=1).astype(bf16)
        all_proj[part] = proj_grad
        term = dot_nt(proj_grad, weights[part, :, : 3 * SPLIT])
        normed_grad = term if normed_grad is None else normed_grad + term
    scale_one = norm_scale(hidden)
    unit = hidden * scale_one
    small_out[0:1, :] = jnp.sum(normed_grad * unit, axis=0, keepdims=True)
    inner = jnp.mean(unit * gain_one * normed_grad, axis=-1, keepdims=True)
    low = (middle_grad + scale_one * (gain_one * normed_grad - unit * inner)).astype(bf16)
    bundle[3 * TOK : 4 * TOK] = low
    bundle[2 * TOK : 3 * TOK] = jnp.concatenate([all_proj[device], context_ref[...]], axis=1)
    flip = jnp.where(iota((TOK, TOK), 0) + iota((TOK, TOK), 1) == TOK - 1, 1.0, 0.0).astype(bf16)
    for head in range(HEADS):
        flipped = dot(flip, all_scores[device * HEADS + head])
        lined = pltpu.roll(flipped, 1, 1, stride=1, stride_axis=0)
        small_out[2 + head : 3 + head, 0:TOK] = jnp.sum(lined, axis=0, keepdims=True)
    bundle[4 * TOK :] = small_out[...].astype(bf16)
    if layer == 1:
        bundle.start()
        sent_out[...] = dot_tn(gated[...], low).astype(bf16)


def weight_grad_kernel(ids, zero, zero_peer, one, one_peer, onehot, out, buffer, sems):
    for layer in range(2):

        @pl.when(ids[0] == layer)
        def _(layer=layer):
            mine, peer = zero, zero_peer
            if layer == 1:
                copies = [pltpu.make_async_copy(x, buffer.at[i], sems.at[i]) for i, x in enumerate((one, one_peer))]
                for copy in copies:
                    copy.start()
                for copy in copies:
                    copy.wait()
                mine, peer = buffer.at[0], buffer.at[1]
            both = [jnp.concatenate([mine[i * TOK : i * TOK + TOK], peer[i * TOK : i * TOK + TOK]], axis=0) for i in range(3)]
            normed, attn, third = both
            left = dot_tn(normed, third[:, : 3 * SPLIT])
            right = dot_tn(attn, third[:, 3 * SPLIT :])
            rows = mine[4 * TOK :].astype(f32) + peer[4 * TOK :].astype(f32)
            lines = rows[:, 0:TOK].astype(bf16)
            keep = (iota((TOK, 16), 1) >= 2) & (iota((TOK, 16), 1) < 5) & (iota((TOK, 16), 0) == iota((TOK, 16), 1))
            lines = dot(jnp.where(keep, 1.0, 0.0).astype(bf16), lines).astype(bf16)
            table = dot_nt(onehot[...], lines)
            tall = jnp.concatenate([rows, jnp.zeros((TOK - 16, WIDTH), f32)], axis=0).T
            lane = iota((WIDTH, TOK), 1)
            extra = jnp.where(lane < 2, tall, table)
            out[...] = jnp.concatenate([left, right, extra], axis=1).astype(bf16).reshape(16, 48, PACK)


def sum_kernel(received, qkv, out_part, gain_one, gain_two, table):
    total = received[0].astype(f32)
    for i in range(1, 16):
        total = total + received[i].astype(f32)
    for c in range(3):
        qkv[c] = total[:, c * SPLIT : (c + 1) * SPLIT]
    out_part[...] = total[:, 3 * SPLIT : WIDTH]
    rows = total[:, WIDTH:].T
    gain_one[...] = rows[0:1, :]
    gain_two[...] = rows[1:2, :]
    table[...] = total[0:2, WIDTH + 2 : WIDTH + 5]


def assemble_kernel(ids, state_zero, state_one, state_zero_peer, state_one_peer, zero, one, zero_peer, one_peer, states, grads):
    rows = slice(3 * TOK, 4 * TOK)
    for item in (state_zero, state_zero_peer, state_one_peer, zero, one, zero_peer, one_peer):
        item.ready()

    @pl.when(ids[0] == 0)
    def _():
        states[0] = state_zero[...]
        states[1] = state_zero_peer[...]
        grads[0] = zero[rows]
        grads[1] = zero_peer[rows]

    @pl.when(ids[0] == 1)
    def _():
        states[0] = state_one_peer[...]
        states[1] = state_one[...]
        grads[0] = one_peer[rows]
        grads[1] = one[rows]


def expert_grad_kernel(ids, *refs):
    layers = (refs[0:4], refs[4:8])
    in_out, out_out, buffer, sems = refs[8:]
    expert = pl.program_id(0)

    @pl.when(expert == 0)
    def _():
        for layer, sources in enumerate(layers):

            @pl.when(ids[0] == layer)
            def _(sources=sources):
                for e in range(2):
                    for i, source in enumerate(sources):
                        pltpu.make_async_copy(source.at[:, e], buffer.at[i, :, e], sems.at[e, i]).start()

    for e in range(2):

        @pl.when(expert == e)
        def _(e=e):
            for i, source in enumerate(layers[0]):
                pltpu.make_async_copy(source.at[:, e], buffer.at[i, :, e], sems.at[e, i]).wait()

    rows, act = [jnp.concatenate([buffer[0, i, expert], buffer[2, i, expert]], axis=0) for i in range(2)]
    pre, back = [jnp.concatenate([buffer[1, i, expert], buffer[3, i, expert]], axis=0) for i in range(2)]
    in_out[0] = dot_tn(rows, pre)
    out_out[0] = dot_tn(act, back)


def after(x, *earlier):
    return lax.optimization_barrier((x, *earlier))[0]


def exchanged(x):
    return lax.all_to_all(x.reshape(16, -1, x.shape[-1]), "dp", 0, 0, tiled=True)


def gathered_mp(x):
    return lax.all_gather(x, "mp", axis=0)


def body(
    inputs, cotangent, segments, buckets, routes, gates, attn_gain, qkv_weight, out_weight, rel_bias, ffn_gain, w_in, w_out
):
    section = lax.axis_index("section")
    ids = jnp.stack([section, lax.axis_index("mp")]).astype(jnp.int32)
    pack, halves = call(
        pack_kernel,
        [((48, PACK), bf16), ((2, 48, 512), bf16)],
        scalars=0,
        load=(0, 1, 2, 3, 4),
        args=(qkv_weight[0].transpose(1, 0, 2), out_weight[0], attn_gain, ffn_gain, rel_bias[0]),
        name="pack",
    )
    spread = call(
        spread_kernel, [((16, 48, 512), bf16)], args=(ids, halves, sent(halves[1], 0)), name="spread"
    )[0]
    w_own = lax.all_gather(pack, ("mp", "dp"), axis=0).reshape(4, WIDTH, PACK)
    in_own, out_own = w_in[0], w_out[0]
    in_other, out_other = swapped(after(in_own, spread)), swapped(after(out_own, spread))
    info = jnp.concatenate(
        [segments.astype(f32)[:, :, None], routes[0].astype(f32), gates[0], jnp.zeros((2, TOK, 3), f32)], axis=2
    )
    info_own = lax.dynamic_index_in_dim(info, section, 0, False)
    info_other = swapped(lax.dynamic_index_in_dim(info, 1 - section, 0, False))
    reverse = jnp.concatenate([buckets[0:1], buckets[1:][::-1]])
    place = jnp.arange(WIDTH, dtype=jnp.int32)
    number = jnp.where(place % 48 < 2, 2 * (place // 48) + place % 48, -1)
    onehot = (number[:, None] == reverse[None, :]).astype(bf16)

    choice = ((TOK, SLOTS), bf16)
    token_shape = ((TOK, WIDTH), bf16)
    sent_shape = ((SLOTS, WIDTH), bf16)
    middle_shape = ((TOK, WIDTH), f32)
    gain_shape = ((8, WIDTH), f32)
    pick_zero, pick_one, gated_zero, gated_one, mask, grad_sent = call(
        prepare_kernel,
        [choice, choice, choice, choice, ((TOK, TOK), f32), sent_shape],
        load=(4,),
        args=(ids, info_own, info_other, segments, cotangent),
        name="prepare",
    )
    half_own = after(exchanged(spread).reshape(WIDTH, 512), mask)
    half_other = swapped(half_own)
    blocks = (16, 2, CAP, WIDTH)
    arrived_one = exchanged(grad_sent).reshape(blocks)
    part_zero, gains_zero = call(
        first_kernel,
        [token_shape, gain_shape],
        load=(1,),
        args=(ids, inputs, half_own, half_other, onehot, mask),
        name="first",
    )
    middle_zero, sent_zero = call(
        dispatch_kernel,
        [middle_shape, sent_shape],
        load=(1,),
        store=(0,),
        args=(ids, inputs, after(gathered_mp(part_zero), arrived_one), gains_zero, pick_zero),
        name="dispatch_zero",
    )
    pair_shape = ((2, 2, 256, WIDTH), bf16)
    received_zero = exchanged(sent_zero).reshape(blocks)
    weights = (in_own, in_other, out_own, out_other)
    expert_scratch = [
        pltpu.VMEM((2, WIDTH, WIDTH), bf16),
        pltpu.VMEM((2, WIDTH, WIDTH), bf16),
        pltpu.SemaphoreType.DMA((2,)),
        pltpu.SemaphoreType.DMA((2,)),
    ]
    y_zero, ahead_zero, slope_zero = call(
        functools.partial(expert_kernel, "forward", 0),
        [(blocks, bf16), pair_shape, ((2, 256, WIDTH), bf16)],
        raw=(2, 3, 4, 5),
        store=(1, 2),
        scratch=expert_scratch,
        args=(ids, received_zero, *weights),
        name="experts_zero",
        limit=20,
    )
    w_own = after(w_own, y_zero)
    w_other = swapped(w_own)

    def combined(matrix, back, name):
        return call(
            combine_kernel, [token_shape], scalars=0, args=(matrix, back.reshape(SLOTS, WIDTH)), name=name
        )[0]

    bias_shape = ((12, TOK, TOK), bf16)
    bias_scratch = [pltpu.VMEM((4, WIDTH, TOK), bf16), pltpu.SemaphoreType.DMA]

    def biased(layer, name):
        return call(
            functools.partial(bias_kernel, layer),
            [bias_shape, gain_shape],
            raw=(1, 2),
            store=(0,),
            scratch=bias_scratch,
            args=(ids, w_own, w_other, onehot, mask),
            name=name,
        )

    bias_one, gains_one = biased(1, "bias_one")
    y_back_zero = after(exchanged(y_zero), gains_one)
    parts_zero = gathered_mp(combined(gated_zero, y_back_zero, "combine_zero"))
    kept_shapes = [token_shape, ((4, TOK, 3 * SPLIT), bf16), bias_shape, ((TOK, SPLIT), bf16)]
    weight_scratch = [pltpu.VMEM((4, WIDTH, WIDTH), bf16), pltpu.SemaphoreType.DMA((4,))]
    forward_scratch = [pltpu.VMEM((4, TOK, SPLIT), bf16)] + weight_scratch
    state_zero, sent_one, middle_one, normed_one, proj_one, probs_one, context_one = call(
        functools.partial(forward_kernel, 1),
        [token_shape, sent_shape, middle_shape] + kept_shapes,
        raw=(3, 4),
        load=(1, 6),
        store=(0, 2, 3, 4, 5, 6),
        scratch=forward_scratch,
        args=(ids, middle_zero, parts_zero, w_own, w_other, gains_one, bias_one, pick_one),
        name="attention_one",
        limit=20,
    )
    bias_zero = biased(0, "bias_zero")[0]
    normed_zero, proj_zero, probs_zero, context_zero = call(
        functools.partial(forward_kernel, 0),
        kept_shapes,
        raw=(2, 3),
        load=(1, 5),
        store=(0, 1, 2, 3),
        scratch=forward_scratch,
        args=(ids, inputs, w_own, after(w_other, sent_one), gains_zero, bias_zero),
        name="attention_zero",
        limit=20,
    )
    received_one = after(exchanged(sent_one).reshape(blocks), normed_zero)
    y_one, buf_one, ahead_one, behind_one = call(
        functools.partial(expert_kernel, "both", 1),
        [(blocks, bf16), (blocks, bf16), pair_shape, pair_shape],
        raw=(3, 4, 5, 6),
        store=(2, 3),
        scratch=expert_scratch,
        args=(ids, received_one, arrived_one, *weights),
        name="experts_one",
        limit=24,
    )
    ahead_zero_peer = sent(ahead_zero, 1)
    ahead_one_peer = sent(ahead_one, 0)
    behind_one_peer = sent(behind_one, 0)
    buf_back_one = exchanged(buf_one)
    y_back_one = exchanged(after(y_one, buf_back_one))
    buf_parts_one = after(gathered_mp(combined(pick_one, buf_back_one, "combine_back_one")), y_back_one)
    y_part_one = combined(gated_one, y_back_one, "combine_one")
    y_parts_one = [y_part_one] + [
        lax.ppermute(y_part_one, "mp", [(i, (i + by) % 4) for i in range(4)]) for by in range(1, 4)
    ]
    grad_scratch = [
        pltpu.VMEM((4, TOK, 3 * SPLIT), bf16),
        pltpu.VMEM((12, TOK, TOK), bf16),
        pltpu.VMEM((16, WIDTH), f32),
    ] + weight_scratch
    back_shape = ((4 * TOK + 16, WIDTH), bf16)
    grad_sent_zero, back_one = call(
        functools.partial(backward_kernel, 1),
        [sent_shape, back_shape],
        raw=(7, 8),
        load=(1, 2, 4, 5, 6, 10, 11),
        store=(1,),
        scratch=grad_scratch,
        args=(
            ids, cotangent, state_zero, buf_parts_one, middle_one, proj_one, probs_one, w_own, w_other, gains_one,
            normed_one, context_one, gated_zero
        ),
        name="attention_back_one",
        limit=24,
    )
    back_one_peer = sent(back_one, 0)
    arrived_zero = exchanged(after(grad_sent_zero, y_part_one)).reshape(blocks)
    state_one = call(
        state_kernel,
        [token_shape],
        load=(1,),
        scratch=[pltpu.VMEM((4, TOK, WIDTH), bf16)],
        args=(ids, middle_one, *y_parts_one),
        name="state_one",
    )[0]
    arrived_zero = after(arrived_zero, ahead_zero_peer, ahead_one_peer, behind_one_peer, *y_parts_one)
    buf_zero, behind_zero = call(
        functools.partial(expert_kernel, "backward", 0),
        [(blocks, bf16), pair_shape],
        raw=(3, 4, 5, 6),
        load=(1,),
        store=(1,),
        scratch=expert_scratch,
        args=(ids, slope_zero, arrived_zero, *weights),
        name="experts_back_zero",
        limit=20,
    )
    state_zero_peer, state_one_peer = sent(state_zero, 1), sent(state_one, 0)
    buf_back_zero = after(exchanged(buf_zero), back_one_peer, state_zero_peer, state_one_peer)
    buf_parts_zero = gathered_mp(combined(pick_zero, buf_back_zero, "combine_back_zero"))
    back_zero = call(
        functools.partial(backward_kernel, 0),
        [back_shape],
        raw=(7, 8),
        load=(1, 2, 4, 5, 6, 10, 11),
        scratch=grad_scratch,
        args=(
            ids, back_one, inputs, buf_parts_zero, middle_zero, proj_zero, probs_zero, w_own, w_other, gains_zero,
            normed_zero, context_zero
        ),
        name="attention_back_zero",
        limit=24,
    )[0]
    back_zero_peer = sent(back_zero, 1)
    packed = call(
        weight_grad_kernel,
        [((16, 48, PACK), bf16)],
        raw=(3, 4),
        scratch=[pltpu.VMEM((2,) + back_shape[0], bf16), pltpu.SemaphoreType.DMA((2,))],
        args=(ids, back_zero, back_zero_peer, back_one, back_one_peer, onehot),
        name="attention_grads",
    )[0]
    shares = exchanged(packed)
    behind_zero_peer = sent(after(behind_zero, packed), 1)
    in_grad, out_grad = pl.pallas_call(
        expert_grad_kernel,
        out_shape=[jax.ShapeDtypeStruct((2, WIDTH, WIDTH), f32)] * 2,
        grid=(2,),
        in_specs=[pl.BlockSpec(memory_space=pltpu.SMEM)] + [pl.BlockSpec(memory_space=pltpu.HBM)] * 8,
        out_specs=[pl.BlockSpec((1, WIDTH, WIDTH), lambda e: (e, 0, 0))] * 2,
        scratch_shapes=[pltpu.VMEM((4, 2, 2, 256, WIDTH), bf16), pltpu.SemaphoreType.DMA((2, 4))],
        compiler_params=pltpu.CompilerParams(vmem_limit_bytes=24 * 1024 * 1024),
        name="expert_grads",
    )(
        ids,
        *map(far, (
        ahead_zero, behind_zero, ahead_zero_peer, behind_zero_peer, ahead_one, behind_one, ahead_one_peer,
        behind_one_peer
        ))
    )
    states, input_grads = call(
        assemble_kernel,
        [((2, TOK, WIDTH), bf16)] * 2,
        load=(1, 3, 4, 5, 6, 7, 8),
        args=(
            ids, state_zero, state_one, state_zero_peer, state_one_peer, back_zero, back_one, back_zero_peer,
            back_one_peer
        ),
        name="assemble",
    )
    qkv_grad, out_grad_part, gain_one_grad, gain_two_grad, table_grad = call(
        sum_kernel,
        [((3, 48, SPLIT), f32), ((48, SPLIT), f32), ((1, 48), f32), ((1, 48), f32), ((2, 3), f32)],
        scalars=0,
        args=(after(shares, in_grad, input_grads),),
        name="sum_grads",
    )
    return (
        states[None],
        input_grads[None],
        gain_one_grad,
        qkv_grad.transpose(1, 0, 2)[None],
        out_grad_part[None],
        table_grad[None],
        gain_two_grad,
        in_grad[None],
        out_grad[None],
    )


def solution(mesh):
    return jax.shard_map(
        body,
        mesh=mesh,
        in_specs=(
            P(None, "dp", None),
            P(None, "dp", None),
            P(None, "dp"),
            P(),
            P("section", None, "dp", None),
            P("section", None, "dp", None),
            P("section", "dp"),
            P("section", "dp", None, "mp"),
            P("section", "dp", "mp"),
            P("section", "dp", "mp"),
            P("section", "dp"),
            P("section", "dp", None, "mp"),
            P("section", "dp", "mp", None),
        ),
        out_specs=(
            P("section", None, "dp", None),
            P("section", None, "dp", None),
            P("section", "dp"),
            P("section", "dp", None, "mp"),
            P("section", "dp", "mp"),
            P("section", "dp", "mp"),
            P("section", "dp"),
            P("section", "dp", None, "mp"),
            P("section", "dp", "mp", None),
        ),
        check_vma=False,
    )
```

```python
import functools

import jax
import jax.numpy as jnp
from jax import lax
from jax.experimental import pallas as pl
from jax.experimental.pallas import tpu as pltpu
from jax.sharding import PartitionSpec as P

bf16 = jnp.bfloat16
f32 = jnp.float32
epsilon = 1e-06
negative = -1e30
root = 0.7978845608028654
cubic = 0.044715
TOK = 128
WIDTH = 768
HEADS = 3
DH = 64
SPLIT = 192
PACK = 896
SLOTS = 512
CAP = 16


def dot(a, b):
    return lax.dot_general(a, b, (((1,), (0,)), ((), ())), preferred_element_type=f32)


def dot_nt(a, b):
    return lax.dot_general(a, b, (((1,), (1,)), ((), ())), preferred_element_type=f32)


def dot_tn(a, b):
    return lax.dot_general(a, b, (((0,), (0,)), ((), ())), preferred_element_type=f32)


def iota(shape, dim):
    return lax.broadcasted_iota(jnp.int32, shape, dim)


def norm_scale(values):
    return lax.rsqrt(jnp.mean(values * values, axis=-1, keepdims=True) + epsilon)


def swapped(x):
    return lax.ppermute(x, "section", [(0, 1), (1, 0)])


def sent(x, source):
    return lax.ppermute(x, "section", [(source, 1 - source)])


class Loaded:
    def __init__(self, source, buffer, sem):
        self.copy = pltpu.make_async_copy(source, buffer, sem)
        self.buffer, self.waiting = buffer, True
        self.copy.start()

    def ready(self):
        if self.waiting:
            self.copy.wait()
            self.waiting = False

    def __getitem__(self, index):
        self.ready()
        return self.buffer[index]


class Stored:
    def __init__(self, target, buffer, sems):
        self.target, self.buffer, self.sems, self.copies = target, buffer, sems, []
        self.dtype = target.dtype

    def __setitem__(self, index, value):
        self.buffer[index] = value

    def start(self, *index):
        source = self.buffer.at[index] if index else self.buffer
        target = self.target.at[index] if index else self.target
        copy = pltpu.make_async_copy(source, target, self.sems.at[len(self.copies)])
        copy.start()
        self.copies.append(copy)

    def finish(self):
        for copy in self.copies:
            copy.wait()


def far(x):
    return pltpu.with_memory_space_constraint(x, pltpu.HBM)


def call(kernel, outs, raw=(), load=(), store=(), scalars=1, scratch=(), args=(), name=None, limit=16):
    specs = []
    for index in range(len(args)):
        if index < scalars:
            specs.append(pl.BlockSpec(memory_space=pltpu.SMEM))
        elif index in raw or index in load:
            specs.append(pl.BlockSpec(memory_space=pltpu.HBM))
        else:
            specs.append(pl.BlockSpec(memory_space=pltpu.VMEM))
    extra = [pltpu.VMEM(args[i].shape, args[i].dtype) for i in load]
    extra += [pltpu.VMEM(*outs[i]) for i in store]
    if load:
        extra.append(pltpu.SemaphoreType.DMA((len(load),)))
    if store:
        extra.append(pltpu.SemaphoreType.DMA((len(store), 8)))

    def wrapped(*refs):
        refs = list(refs)
        count = len(args) + len(outs)
        own = refs[count : len(refs) - len(extra)]
        more = refs[len(refs) - len(extra) :]
        load_sems = more[len(load) + len(store)] if load else None
        store_sems = more[-1] if store else None
        for n, i in enumerate(load):
            refs[i] = Loaded(refs[i], more[n], load_sems.at[n])
        stored = []
        for n, i in enumerate(store):
            refs[len(args) + i] = Stored(refs[len(args) + i], more[len(load) + n], store_sems.at[n])
            stored.append(refs[len(args) + i])
        kernel(*refs[:count], *own)
        for item in refs[:count]:
            if isinstance(item, Loaded):
                item.ready()
        for item in stored:
            if not item.copies:
                item.start()
        for item in stored:
            item.finish()

    args = [far(x) if i in raw or i in load else x for i, x in enumerate(args)]
    return pl.pallas_call(
        wrapped,
        out_shape=[
            pltpu.HBM(shape, dtype) if i in store else jax.ShapeDtypeStruct(shape, dtype)
            for i, (shape, dtype) in enumerate(outs)
        ],
        in_specs=specs,
        out_specs=[
            pl.BlockSpec(memory_space=pltpu.HBM if i in store else pltpu.VMEM) for i in range(len(outs))
        ],
        scratch_shapes=list(scratch) + extra,
        compiler_params=pltpu.CompilerParams(vmem_limit_bytes=limit * 1024 * 1024),
        name=name,
    )(*args)


def fetch(here, own, other, buffer, sems):
    count = buffer.shape[0]
    lanes = pl.ds(0, WIDTH)

    @pl.when(here)
    def _():
        for i in range(count):
            pltpu.make_async_copy(own.at[i, :, lanes], buffer.at[i], sems.at[i]).start()

    @pl.when(jnp.logical_not(here))
    def _():
        for i in range(count):
            pltpu.make_async_copy(other.at[i, :, lanes], buffer.at[i], sems.at[i]).start()

    def arrived(start=0, stop=count):
        for i in range(start, stop):
            pltpu.make_async_copy(own.at[i, :, lanes], buffer.at[i], sems.at[i]).wait()

    return arrived


def pack_kernel(qkv, out_part, gain_one, gain_two, table, whole, halves):
    eye = iota((48, 48), 0) == iota((48, 48), 1)
    one = jnp.sum(jnp.where(eye, gain_one[...].astype(f32), 0.0), axis=1, keepdims=True)
    two = jnp.sum(jnp.where(eye, gain_two[...].astype(f32), 0.0), axis=1, keepdims=True)
    row, lane = iota((48, TOK), 0), iota((48, TOK), 1)
    extra = jnp.where(lane == 0, one, jnp.where(lane == 1, two, 0.0))
    values = table[...].astype(f32)
    for r in range(2):
        for h in range(HEADS):
            extra = extra + jnp.where((row == r) & (lane == 2 + h), values[r : r + 1, h : h + 1], 0.0)
    parts = [qkv[0], qkv[1], qkv[2], out_part[...]]
    line = jnp.concatenate(parts + [extra.astype(bf16), jnp.zeros((48, TOK), bf16)], axis=1)
    whole[...] = line[:, :PACK]
    halves[0] = line[:, :512]
    halves[1] = line[:, 512:]


def spread_kernel(ids, halves, received, out):
    chosen = jnp.where(ids[0] == 0, halves[0], received[...])
    for i in range(16):
        out[i] = chosen


def first_kernel(ids, inputs, own, other, onehot, mask, part_out, gains_out):
    first = ids[0] == 0
    hidden = jnp.where(first, inputs[0], inputs[1]).astype(f32)
    scaled = hidden * norm_scale(hidden)
    low = jnp.where(first, own[...], other[...])
    high = jnp.where(first, other[...], own[...])
    weight = jnp.concatenate([low, high], axis=1)
    rows = weight[:, WIDTH:PACK].astype(f32).T
    gains_out[...] = rows[0:8]
    normed = (scaled * rows[0:1]).astype(bf16)
    proj = dot(normed, weight[:, : 3 * SPLIT]).astype(bf16)
    line = dot_tn(weight[:, WIDTH:PACK], onehot[...]).astype(bf16)
    allowed = mask[...] > 0.5
    pieces = [jnp.zeros((TOK, DH), bf16)]
    for head in range(HEADS):
        probs, value = head_probs(proj, head_bias(line, allowed, head), head)
        pieces.append(dot(probs, value).astype(bf16))
    part_out[...] = dot_nt(jnp.concatenate(pieces, axis=1), weight[:, 512:WIDTH]).astype(bf16)


def dispatch_kernel(ids, inputs, parts, gain_rows, pick, middle_out, sent_out):
    hidden = jnp.where(ids[0] == 0, inputs[0], inputs[1]).astype(f32)
    for i in range(4):
        hidden = hidden + parts[i].astype(f32)
    middle_out[...] = hidden
    normed = (hidden * norm_scale(hidden) * gain_rows[1:2, :]).astype(bf16)
    sent_out[...] = dot_tn(pick[...], normed).astype(bf16)


def prepare_kernel(ids, own, other, segments, cotangent, pick_zero, pick_one, gated_zero, gated_one, mask, sent_grad):
    section = ids[0]
    first = section == 0
    row = jnp.where(first, segments[0:1, :], segments[1:2, :]).astype(f32)
    column = own[:, 0:1]
    causal = iota((TOK, TOK), 0) >= iota((TOK, TOK), 1)
    mask[...] = jnp.where(causal & (column == row), 1.0, 0.0)
    expert = iota((TOK, 32), 1).astype(f32)
    lower = jnp.where(iota((TOK, TOK), 0) > iota((TOK, TOK), 1), 1.0, 0.0).astype(bf16)
    spread = jnp.where(lax.shift_right_logical(iota((32, SLOTS), 1), 4) == iota((32, SLOTS), 0), 1.0, 0.0).astype(bf16)
    slot = iota((TOK, SLOTS), 1)
    slot_expert = lax.shift_right_logical(slot, 4).astype(f32)
    slot_place = (slot & 15).astype(f32)
    for layer in range(2):
        info = jnp.where(section == layer, own[...], other[...])
        r0, r1, g0, g1 = info[:, 1:2], info[:, 2:3], info[:, 3:4], info[:, 4:5]
        named = jnp.where((r0 == expert) | (r1 == expert), 1.0, 0.0).astype(bf16)
        earlier = dot(lower, named)
        here = dot(earlier.astype(bf16), spread) == slot_place
        d0 = here & (r0 == slot_expert)
        d1 = here & (r1 == slot_expert)
        (pick_zero, pick_one)[layer][...] = jnp.where(d0 | d1, 1.0, 0.0).astype(bf16)
        gates = jnp.where(d0, g0, jnp.where(d1, g1, 0.0)).astype(bf16)
        (gated_zero, gated_one)[layer][...] = gates
        if layer == 1:
            grad = jnp.where(first, cotangent[0], cotangent[1])
            sent_grad[...] = dot_tn(gates, grad).astype(bf16)


def head_bias(line, allowed, head):
    chosen = jnp.where(iota((TOK, TOK), 1) == 2 + head, 1.0, 0.0).astype(bf16)
    bias = pltpu.roll(dot(chosen, line), 0, 1, stride=1, stride_axis=0)
    return jnp.where(allowed, bias, negative)


def head_probs(proj, bias, head):
    at = head * DH
    query = proj[:, at : at + DH]
    key = proj[:, SPLIT + at : SPLIT + at + DH]
    value = proj[:, 2 * SPLIT + at : 2 * SPLIT + at + DH]
    scores = dot_nt(query * jnp.asarray(0.125, bf16), key) + bias
    peak = jnp.max(scores, axis=-1, keepdims=True)
    expos = jnp.exp(scores - peak)
    return (expos / jnp.sum(expos, axis=-1, keepdims=True)).astype(bf16), value


def bias_kernel(layer, ids, own, other, onehot, mask, bias_out, gains_out, extra, sem):
    lanes = pl.ds(WIDTH, TOK)

    @pl.when(ids[0] == layer)
    def _():
        pltpu.make_async_copy(own.at[:, :, lanes], extra, sem).start()

    @pl.when(ids[0] != layer)
    def _():
        pltpu.make_async_copy(other.at[:, :, lanes], extra, sem).start()

    pltpu.make_async_copy(own.at[:, :, lanes], extra, sem).wait()
    gains_out[...] = extra[0].astype(f32).T[0:8]
    allowed = mask[...] > 0.5
    for part in range(4):
        line = dot_tn(extra[part], onehot[...]).astype(bf16)
        for head in range(HEADS):
            bias_out[part * HEADS + head] = head_bias(line, allowed, head).astype(bf16)


def forward_kernel(layer, ids, *refs):
    if layer == 0:
        inputs, own, other, gain_rows, bias = refs[:5]
        rest = refs[5:]
    else:
        before, parts, own, other, gain_rows, bias, pick, state_out, sent_out, middle_out = refs[:10]
        rest = refs[10:]
    normed_out, proj_out, probs_out, context_out, contexts, weights, sems = rest
    section = ids[0]
    arrived = fetch(section == layer, own, other, weights, sems)
    if layer == 0:
        hidden = jnp.where(section == 0, inputs[0], inputs[1]).astype(f32)
    else:
        added = parts[0].astype(f32)
        for i in range(1, 4):
            added = added + parts[i].astype(f32)
        state = (before[...] + added).astype(bf16)
        state_out[...] = state
        state_out.start()
        hidden = state.astype(f32)
    normed = (hidden * norm_scale(hidden) * gain_rows[0:1, :]).astype(bf16)
    normed_out[...] = normed
    normed_out.start()
    attn = None
    for part in range(4):
        if part % 2 == 0:
            arrived(part, part + 2)
        proj = dot(normed, weights[part, :, : 3 * SPLIT]).astype(bf16)
        proj_out[part] = proj
        proj_out.start(part)
        pieces = []
        for head in range(HEADS):
            probs, value = head_probs(proj, bias[part * HEADS + head].astype(f32), head)
            probs_out[part * HEADS + head] = probs
            pieces.append(dot(probs, value).astype(bf16))
        probs_out.start(pl.ds(part * HEADS, HEADS))
        contexts[part] = jnp.concatenate(pieces, axis=1)
        if layer == 1:
            padded = jnp.concatenate([jnp.zeros((TOK, DH), bf16)] + pieces, axis=1)
            term = dot_nt(padded, weights[part, :, 512:WIDTH])
            attn = term if attn is None else attn + term
    context_out[...] = contexts[ids[1]]
    context_out.start()
    if layer == 1:
        middle = hidden + attn
        middle_out[...] = middle
        middle_out.start()
        normed_two = (middle * norm_scale(middle) * gain_rows[1:2, :]).astype(bf16)
        sent_out[...] = dot_tn(pick[...], normed_two).astype(bf16)


def gelu_both(x):
    square = x * x
    th = jnp.tanh(root * (x + cubic * x * square))
    half = 0.5 * (1.0 + th)
    value = x * half
    slope = half + 0.5 * x * (1.0 - th * th) * (root * (1.0 + 3.0 * cubic * square))
    return value, slope


def rows_of(ref, expert):
    return ref[:, expert].reshape(256, WIDTH)


def expert_kernel(mode, layer, ids, *refs):
    if mode == "forward":
        received, in_own, in_other, out_own, out_other, y_out, ahead, slope_out = refs[:8]
    elif mode == "both":
        received, arrived_grad, in_own, in_other, out_own, out_other, y_out, buf_out, ahead, behind = refs[:10]
    else:
        slope_in, arrived_grad, in_own, in_other, out_own, out_other, buf_out, behind = refs[:8]
    w_in, w_out, in_sems, out_sems = refs[-4:]
    here = ids[0] == layer
    if mode != "forward":
        backs = [rows_of(arrived_grad, e) for e in range(2)]
    if mode == "backward":
        out_arrived = fetch(here, out_own, out_other, w_out, out_sems)
        in_arrived = fetch(here, in_own, in_other, w_in, in_sems)
        slopes = [slope_in[e].astype(f32) for e in range(2)]
        for e in range(2):
            behind[1, e] = backs[e]
        behind.start(1)
        out_arrived()
    else:
        in_arrived = fetch(here, in_own, in_other, w_in, in_sems)
        out_arrived = fetch(here, out_own, out_other, w_out, out_sems)
        acts, slopes = [], []
        for e in range(2):
            ahead[0, e] = rows_of(received, e)
        ahead.start(0)
        if mode == "both":
            for e in range(2):
                behind[1, e] = backs[e]
            behind.start(1)
        in_arrived()
        for e in range(2):
            rows = rows_of(received, e)
            value, slope = gelu_both(dot(rows, w_in[e]))
            acts.append(value.astype(bf16))
            slopes.append(slope)
            ahead[1, e] = acts[e]
            if mode == "forward":
                slope_out[e] = slope.astype(bf16)
        ahead.start(1)
        if mode == "forward":
            slope_out.start()
        out_arrived()
        for e in range(2):
            y_out[:, e] = dot(acts[e], w_out[e]).astype(bf16).reshape(16, CAP, WIDTH)
    if mode != "forward":
        pres = []
        for e in range(2):
            pres.append((dot_nt(backs[e], w_out[e]) * slopes[e]).astype(bf16))
            behind[0, e] = pres[e]
        behind.start(0)
        if mode == "backward":
            in_arrived()
        for e in range(2):
            buf_out[:, e] = dot_nt(pres[e], w_in[e]).astype(bf16).reshape(16, CAP, WIDTH)


def combine_kernel(matrix, returned, out):
    out[...] = dot(matrix[...], returned[...]).astype(out.dtype)


def state_kernel(ids, before, *refs):
    parts, out, ordered = refs[:4], refs[4], refs[5]
    for by in range(4):
        ordered[(ids[1] + 4 - by) & 3] = parts[by][...]
    total = before[...]
    for i in range(4):
        total = total + ordered[i].astype(f32)
    out[...] = total.astype(bf16)


def backward_kernel(layer, ids, *refs):
    if layer == 1:
        grads, hidden_ref = refs[0], refs[1]
    else:
        grads, hidden_ref = refs[0], refs[1]
    parts, middle_ref, proj_ref, probs_ref, own, other, gain_rows, normed_ref, context_ref = refs[2:11]
    rest = refs[11:]
    if layer == 1:
        gated, rest = rest[0], rest[1:]
    if layer == 1:
        sent_out, rest = rest[0], rest[1:]
    bundle, all_proj, all_scores, small_out, weights, sems = rest
    arrived = fetch(ids[0] == layer, own, other, weights, sems)
    section = ids[0]
    device = ids[1]
    first = section == 0
    if layer == 1:
        grad = jnp.where(first, grads[0], grads[1]).astype(f32)
        hidden = hidden_ref[...].astype(f32)
    else:
        grad = grads[3 * TOK : 4 * TOK].astype(f32)
        hidden = jnp.where(first, hidden_ref[0], hidden_ref[1]).astype(f32)
    middle = middle_ref[...]
    buf = parts[0].astype(f32)
    for i in range(1, 4):
        buf = buf + parts[i].astype(f32)
    scale_two = norm_scale(middle)
    gain_one, gain_two = gain_rows[0:1, :], gain_rows[1:2, :]
    small_out[...] = jnp.zeros(small_out.shape, f32)
    unit = middle * scale_two
    small_out[1:2, :] = jnp.sum(buf * unit, axis=0, keepdims=True)
    inner = jnp.mean(unit * gain_two * buf, axis=-1, keepdims=True)
    middle_grad = grad + scale_two * (gain_two * buf - unit * inner)
    attn_low = middle_grad.astype(bf16)
    bundle[0:TOK] = normed_ref[...]
    bundle[TOK : 2 * TOK] = attn_low
    normed_grad = None
    for part in range(4):
        if part % 2 == 0:
            arrived(part, part + 2)
        context_grad = dot(attn_low, weights[part, :, 512:WIDTH]).astype(bf16)
        proj = proj_ref[part]
        q_parts, k_parts, v_parts = [], [], []
        for head in range(HEADS):
            at = head * DH
            query = proj[:, at : at + DH]
            key = proj[:, SPLIT + at : SPLIT + at + DH]
            value = proj[:, 2 * SPLIT + at : 2 * SPLIT + at + DH]
            probs = probs_ref[part * HEADS + head]
            back = context_grad[:, DH + at : DH + at + DH]
            wide = probs.astype(f32)
            prob_grad = dot_nt(back, value)
            inner = jnp.sum(wide * prob_grad, axis=-1, keepdims=True)
            score_grad = (wide * (prob_grad - inner)).astype(bf16)
            all_scores[part * HEADS + head] = score_grad
            q_parts.append(dot(score_grad, key) * 0.125)
            k_parts.append(dot_tn(score_grad, query) * 0.125)
            v_parts.append(dot_tn(probs, back))
        proj_grad = jnp.concatenate(q_parts + k_parts + v_parts, axis=1).astype(bf16)
        all_proj[part] = proj_grad
        term = dot_nt(proj_grad, weights[part, :, : 3 * SPLIT])
        normed_grad = term if normed_grad is None else normed_grad + term
    scale_one = norm_scale(hidden)
    unit = hidden * scale_one
    small_out[0:1, :] = jnp.sum(normed_grad * unit, axis=0, keepdims=True)
    inner = jnp.mean(unit * gain_one * normed_grad, axis=-1, keepdims=True)
    low = (middle_grad + scale_one * (gain_one * normed_grad - unit * inner)).astype(bf16)
    bundle[3 * TOK : 4 * TOK] = low
    bundle[2 * TOK : 3 * TOK] = jnp.concatenate([all_proj[device], context_ref[...]], axis=1)
    flip = jnp.where(iota((TOK, TOK), 0) + iota((TOK, TOK), 1) == TOK - 1, 1.0, 0.0).astype(bf16)
    for head in range(HEADS):
        flipped = dot(flip, all_scores[device * HEADS + head])
        lined = pltpu.roll(flipped, 1, 1, stride=1, stride_axis=0)
        small_out[2 + head : 3 + head, 0:TOK] = jnp.sum(lined, axis=0, keepdims=True)
    bundle[4 * TOK :] = small_out[...].astype(bf16)
    if layer == 1:
        bundle.start()
        sent_out[...] = dot_tn(gated[...], low).astype(bf16)


def weight_grad_kernel(ids, zero, zero_peer, one, one_peer, onehot, out, buffer, sems):
    for layer in range(2):

        @pl.when(ids[0] == layer)
        def _(layer=layer):
            mine, peer = zero, zero_peer
            if layer == 1:
                copies = [pltpu.make_async_copy(x, buffer.at[i], sems.at[i]) for i, x in enumerate((one, one_peer))]
                for copy in copies:
                    copy.start()
                for copy in copies:
                    copy.wait()
                mine, peer = buffer.at[0], buffer.at[1]
            both = [jnp.concatenate([mine[i * TOK : i * TOK + TOK], peer[i * TOK : i * TOK + TOK]], axis=0) for i in range(3)]
            normed, attn, third = both
            left = dot_tn(normed, third[:, : 3 * SPLIT])
            right = dot_tn(attn, third[:, 3 * SPLIT :])
            rows = mine[4 * TOK :].astype(f32) + peer[4 * TOK :].astype(f32)
            lines = rows[:, 0:TOK].astype(bf16)
            keep = (iota((TOK, 16), 1) >= 2) & (iota((TOK, 16), 1) < 5) & (iota((TOK, 16), 0) == iota((TOK, 16), 1))
            lines = dot(jnp.where(keep, 1.0, 0.0).astype(bf16), lines).astype(bf16)
            table = dot_nt(onehot[...], lines)
            tall = jnp.concatenate([rows, jnp.zeros((TOK - 16, WIDTH), f32)], axis=0).T
            lane = iota((WIDTH, TOK), 1)
            extra = jnp.where(lane < 2, tall, table)
            out[...] = jnp.concatenate([left, right, extra], axis=1).astype(bf16).reshape(16, 48, PACK)


def sum_kernel(received, qkv, out_part, gain_one, gain_two, table):
    total = received[0].astype(f32)
    for i in range(1, 16):
        total = total + received[i].astype(f32)
    for c in range(3):
        qkv[c] = total[:, c * SPLIT : (c + 1) * SPLIT]
    out_part[...] = total[:, 3 * SPLIT : WIDTH]
    rows = total[:, WIDTH:].T
    gain_one[...] = rows[0:1, :]
    gain_two[...] = rows[1:2, :]
    table[...] = total[0:2, WIDTH + 2 : WIDTH + 5]


def assemble_kernel(ids, state_zero, state_one, state_zero_peer, state_one_peer, zero, one, zero_peer, one_peer, states, grads):
    rows = slice(3 * TOK, 4 * TOK)
    for item in (state_zero, state_zero_peer, state_one_peer, zero, one, zero_peer, one_peer):
        item.ready()

    @pl.when(ids[0] == 0)
    def _():
        states[0] = state_zero[...]
        states[1] = state_zero_peer[...]
        grads[0] = zero[rows]
        grads[1] = zero_peer[rows]

    @pl.when(ids[0] == 1)
    def _():
        states[0] = state_one_peer[...]
        states[1] = state_one[...]
        grads[0] = one_peer[rows]
        grads[1] = one[rows]


def expert_grad_kernel(ids, *refs):
    layers = (refs[0:4], refs[4:8])
    in_out, out_out, buffer, sems = refs[8:]
    expert = pl.program_id(0)

    @pl.when(expert == 0)
    def _():
        for layer, sources in enumerate(layers):

            @pl.when(ids[0] == layer)
            def _(sources=sources):
                for e in range(2):
                    for i, source in enumerate(sources):
                        pltpu.make_async_copy(source.at[:, e], buffer.at[i, :, e], sems.at[e, i]).start()

    for e in range(2):

        @pl.when(expert == e)
        def _(e=e):
            for i, source in enumerate(layers[0]):
                pltpu.make_async_copy(source.at[:, e], buffer.at[i, :, e], sems.at[e, i]).wait()

    rows, act = [jnp.concatenate([buffer[0, i, expert], buffer[2, i, expert]], axis=0) for i in range(2)]
    pre, back = [jnp.concatenate([buffer[1, i, expert], buffer[3, i, expert]], axis=0) for i in range(2)]
    in_out[0] = dot_tn(rows, pre)
    out_out[0] = dot_tn(act, back)


def after(x, *earlier):
    return lax.optimization_barrier((x, *earlier))[0]


def exchanged(x):
    return lax.all_to_all(x.reshape(16, -1, x.shape[-1]), "dp", 0, 0, tiled=True)


def gathered_mp(x):
    return lax.all_gather(x, "mp", axis=0)


def body(
    inputs, cotangent, segments, buckets, routes, gates, attn_gain, qkv_weight, out_weight, rel_bias, ffn_gain, w_in, w_out
):
    section = lax.axis_index("section")
    ids = jnp.stack([section, lax.axis_index("mp")]).astype(jnp.int32)
    pack, halves = call(
        pack_kernel,
        [((48, PACK), bf16), ((2, 48, 512), bf16)],
        scalars=0,
        load=(0, 1, 2, 3, 4),
        args=(qkv_weight[0].transpose(1, 0, 2), out_weight[0], attn_gain, ffn_gain, rel_bias[0]),
        name="pack",
    )
    spread = call(
        spread_kernel, [((16, 48, 512), bf16)], args=(ids, halves, sent(halves[1], 0)), name="spread"
    )[0]
    w_own = lax.all_gather(pack, ("mp", "dp"), axis=0).reshape(4, WIDTH, PACK)
    in_own, out_own = w_in[0], w_out[0]
    in_other, out_other = swapped(after(in_own, spread)), swapped(after(out_own, spread))
    info = jnp.concatenate(
        [segments.astype(f32)[:, :, None], routes[0].astype(f32), gates[0], jnp.zeros((2, TOK, 3), f32)], axis=2
    )
    info_own = lax.dynamic_index_in_dim(info, section, 0, False)
    info_other = swapped(lax.dynamic_index_in_dim(info, 1 - section, 0, False))
    reverse = jnp.concatenate([buckets[0:1], buckets[1:][::-1]])
    place = jnp.arange(WIDTH, dtype=jnp.int32)
    number = jnp.where(place % 48 < 2, 2 * (place // 48) + place % 48, -1)
    onehot = (number[:, None] == reverse[None, :]).astype(bf16)

    choice = ((TOK, SLOTS), bf16)
    token_shape = ((TOK, WIDTH), bf16)
    sent_shape = ((SLOTS, WIDTH), bf16)
    middle_shape = ((TOK, WIDTH), f32)
    gain_shape = ((8, WIDTH), f32)
    pick_zero, pick_one, gated_zero, gated_one, mask, grad_sent = call(
        prepare_kernel,
        [choice, choice, choice, choice, ((TOK, TOK), f32), sent_shape],
        load=(4,),
        args=(ids, info_own, info_other, segments, cotangent),
        name="prepare",
    )
    half_own = after(exchanged(spread).reshape(WIDTH, 512), mask)
    half_other = swapped(half_own)
    blocks = (16, 2, CAP, WIDTH)
    arrived_one = exchanged(grad_sent).reshape(blocks)
    part_zero, gains_zero = call(
        first_kernel,
        [token_shape, gain_shape],
        load=(1,),
        args=(ids, inputs, half_own, half_other, onehot, mask),
        name="first",
    )
    middle_zero, sent_zero = call(
        dispatch_kernel,
        [middle_shape, sent_shape],
        load=(1,),
        store=(0,),
        args=(ids, inputs, after(gathered_mp(part_zero), arrived_one), gains_zero, pick_zero),
        name="dispatch_zero",
    )
    pair_shape = ((2, 2, 256, WIDTH), bf16)
    received_zero = exchanged(sent_zero).reshape(blocks)
    weights = (in_own, in_other, out_own, out_other)
    expert_scratch = [
        pltpu.VMEM((2, WIDTH, WIDTH), bf16),
        pltpu.VMEM((2, WIDTH, WIDTH), bf16),
        pltpu.SemaphoreType.DMA((2,)),
        pltpu.SemaphoreType.DMA((2,)),
    ]
    y_zero, ahead_zero, slope_zero = call(
        functools.partial(expert_kernel, "forward", 0),
        [(blocks, bf16), pair_shape, ((2, 256, WIDTH), bf16)],
        raw=(2, 3, 4, 5),
        store=(1, 2),
        scratch=expert_scratch,
        args=(ids, received_zero, *weights),
        name="experts_zero",
        limit=20,
    )
    w_own = after(w_own, y_zero)
    w_other = swapped(w_own)

    def combined(matrix, back, name):
        return call(
            combine_kernel, [token_shape], scalars=0, args=(matrix, back.reshape(SLOTS, WIDTH)), name=name
        )[0]

    bias_shape = ((12, TOK, TOK), bf16)
    bias_scratch = [pltpu.VMEM((4, WIDTH, TOK), bf16), pltpu.SemaphoreType.DMA]

    def biased(layer, name):
        return call(
            functools.partial(bias_kernel, layer),
            [bias_shape, gain_shape],
            raw=(1, 2),
            store=(0,),
            scratch=bias_scratch,
            args=(ids, w_own, w_other, onehot, mask),
            name=name,
        )

    bias_one, gains_one = biased(1, "bias_one")
    y_back_zero = after(exchanged(y_zero), gains_one)
    parts_zero = gathered_mp(combined(gated_zero, y_back_zero, "combine_zero"))
    kept_shapes = [token_shape, ((4, TOK, 3 * SPLIT), bf16), bias_shape, ((TOK, SPLIT), bf16)]
    weight_scratch = [pltpu.VMEM((4, WIDTH, WIDTH), bf16), pltpu.SemaphoreType.DMA((4,))]
    forward_scratch = [pltpu.VMEM((4, TOK, SPLIT), bf16)] + weight_scratch
    state_zero, sent_one, middle_one, normed_one, proj_one, probs_one, context_one = call(
        functools.partial(forward_kernel, 1),
        [token_shape, sent_shape, middle_shape] + kept_shapes,
        raw=(3, 4),
        load=(1, 6),
        store=(0, 2, 3, 4, 5, 6),
        scratch=forward_scratch,
        args=(ids, middle_zero, parts_zero, w_own, w_other, gains_one, bias_one, pick_one),
        name="attention_one",
        limit=20,
    )
    bias_zero = biased(0, "bias_zero")[0]
    normed_zero, proj_zero, probs_zero, context_zero = call(
        functools.partial(forward_kernel, 0),
        kept_shapes,
        raw=(2, 3),
        load=(1, 5),
        store=(0, 1, 2, 3),
        scratch=forward_scratch,
        args=(ids, inputs, w_own, after(w_other, sent_one), gains_zero, bias_zero),
        name="attention_zero",
        limit=20,
    )
    received_one = after(exchanged(sent_one).reshape(blocks), normed_zero)
    y_one, buf_one, ahead_one, behind_one = call(
        functools.partial(expert_kernel, "both", 1),
        [(blocks, bf16), (blocks, bf16), pair_shape, pair_shape],
        raw=(3, 4, 5, 6),
        store=(2, 3),
        scratch=expert_scratch,
        args=(ids, received_one, arrived_one, *weights),
        name="experts_one",
        limit=24,
    )
    ahead_zero_peer = sent(ahead_zero, 1)
    ahead_one_peer = sent(ahead_one, 0)
    behind_one_peer = sent(behind_one, 0)
    buf_back_one = exchanged(buf_one)
    y_back_one = exchanged(after(y_one, buf_back_one))
    buf_parts_one = after(gathered_mp(combined(pick_one, buf_back_one, "combine_back_one")), y_back_one)
    y_part_one = combined(gated_one, y_back_one, "combine_one")
    y_parts_one = [y_part_one] + [
        lax.ppermute(y_part_one, "mp", [(i, (i + by) % 4) for i in range(4)]) for by in range(1, 4)
    ]
    grad_scratch = [
        pltpu.VMEM((4, TOK, 3 * SPLIT), bf16),
        pltpu.VMEM((12, TOK, TOK), bf16),
        pltpu.VMEM((16, WIDTH), f32),
    ] + weight_scratch
    back_shape = ((4 * TOK + 16, WIDTH), bf16)
    grad_sent_zero, back_one = call(
        functools.partial(backward_kernel, 1),
        [sent_shape, back_shape],
        raw=(7, 8),
        load=(1, 2, 4, 5, 6, 10, 11),
        store=(1,),
        scratch=grad_scratch,
        args=(
            ids, cotangent, state_zero, buf_parts_one, middle_one, proj_one, probs_one, w_own, w_other, gains_one,
            normed_one, context_one, gated_zero
        ),
        name="attention_back_one",
        limit=24,
    )
    back_one_peer = sent(back_one, 0)
    arrived_zero = exchanged(after(grad_sent_zero, y_part_one)).reshape(blocks)
    state_one = call(
        state_kernel,
        [token_shape],
        load=(1,),
        scratch=[pltpu.VMEM((4, TOK, WIDTH), bf16)],
        args=(ids, middle_one, *y_parts_one),
        name="state_one",
    )[0]
    arrived_zero = after(arrived_zero, ahead_zero_peer, ahead_one_peer, behind_one_peer, *y_parts_one)
    buf_zero, behind_zero = call(
        functools.partial(expert_kernel, "backward", 0),
        [(blocks, bf16), pair_shape],
        raw=(3, 4, 5, 6),
        load=(1,),
        store=(1,),
        scratch=expert_scratch,
        args=(ids, slope_zero, arrived_zero, *weights),
        name="experts_back_zero",
        limit=20,
    )
    state_zero_peer, state_one_peer = sent(state_zero, 1), sent(state_one, 0)
    behind_zero_peer = sent(after(behind_zero, state_one), 1)
    buf_back_zero = after(exchanged(buf_zero), back_one_peer, state_zero_peer, state_one_peer, behind_zero_peer)
    buf_parts_zero = gathered_mp(combined(pick_zero, buf_back_zero, "combine_back_zero"))
    back_zero = call(
        functools.partial(backward_kernel, 0),
        [back_shape],
        raw=(7, 8),
        load=(1, 2, 4, 5, 6, 10, 11),
        scratch=grad_scratch,
        args=(
            ids, back_one, inputs, buf_parts_zero, middle_zero, proj_zero, probs_zero, w_own, w_other, gains_zero,
            normed_zero, context_zero
        ),
        name="attention_back_zero",
        limit=24,
    )[0]
    back_zero_peer = sent(back_zero, 1)
    packed = call(
        weight_grad_kernel,
        [((16, 48, PACK), bf16)],
        raw=(3, 4),
        scratch=[pltpu.VMEM((2,) + back_shape[0], bf16), pltpu.SemaphoreType.DMA((2,))],
        args=(ids, back_zero, back_zero_peer, back_one, back_one_peer, onehot),
        name="attention_grads",
    )[0]
    shares = exchanged(packed)
    in_grad, out_grad = pl.pallas_call(
        expert_grad_kernel,
        out_shape=[jax.ShapeDtypeStruct((2, WIDTH, WIDTH), f32)] * 2,
        grid=(2,),
        in_specs=[pl.BlockSpec(memory_space=pltpu.SMEM)] + [pl.BlockSpec(memory_space=pltpu.HBM)] * 8,
        out_specs=[pl.BlockSpec((1, WIDTH, WIDTH), lambda e: (e, 0, 0))] * 2,
        scratch_shapes=[pltpu.VMEM((4, 2, 2, 256, WIDTH), bf16), pltpu.SemaphoreType.DMA((2, 4))],
        compiler_params=pltpu.CompilerParams(vmem_limit_bytes=24 * 1024 * 1024),
        name="expert_grads",
    )(
        ids,
        *map(far, (
        ahead_zero, behind_zero, ahead_zero_peer, behind_zero_peer, ahead_one, behind_one, ahead_one_peer,
        behind_one_peer
        ))
    )
    states, input_grads = call(
        assemble_kernel,
        [((2, TOK, WIDTH), bf16)] * 2,
        load=(1, 3, 4, 5, 6, 7, 8),
        args=(
            ids, state_zero, state_one, state_zero_peer, state_one_peer, back_zero, back_one, back_zero_peer,
            back_one_peer
        ),
        name="assemble",
    )
    qkv_grad, out_grad_part, gain_one_grad, gain_two_grad, table_grad = call(
        sum_kernel,
        [((3, 48, SPLIT), f32), ((48, SPLIT), f32), ((1, 48), f32), ((1, 48), f32), ((2, 3), f32)],
        scalars=0,
        args=(after(shares, in_grad, input_grads),),
        name="sum_grads",
    )
    return (
        states[None],
        input_grads[None],
        gain_one_grad,
        qkv_grad.transpose(1, 0, 2)[None],
        out_grad_part[None],
        table_grad[None],
        gain_two_grad,
        in_grad[None],
        out_grad[None],
    )


def solution(mesh):
    return jax.shard_map(
        body,
        mesh=mesh,
        in_specs=(
            P(None, "dp", None),
            P(None, "dp", None),
            P(None, "dp"),
            P(),
            P("section", None, "dp", None),
            P("section", None, "dp", None),
            P("section", "dp"),
            P("section", "dp", None, "mp"),
            P("section", "dp", "mp"),
            P("section", "dp", "mp"),
            P("section", "dp"),
            P("section", "dp", None, "mp"),
            P("section", "dp", "mp", None),
        ),
        out_specs=(
            P("section", None, "dp", None),
            P("section", None, "dp", None),
            P("section", "dp"),
            P("section", "dp", None, "mp"),
            P("section", "dp", "mp"),
            P("section", "dp", "mp"),
            P("section", "dp"),
            P("section", "dp", None, "mp"),
            P("section", "dp", "mp", None),
        ),
        check_vma=False,
    )
```
